256 devices in a mesh: wall: 8 (over y, core), surf: 32 (over x, z).
Axes of the slice: x: 4, y: 4, z: 8, core: 2. Of those that a mesh axis runs over, the one named last changes fastest.
Arguments:
- vector: bfloat16 [128, 32, 320, 256], P('surf', 'wall'), may hold values from -40 to 40
- lengths: int32 [128], P('surf'), may hold values from 1 to 32, as said below
- north_of: int32 [32, 4], P('surf'), may hold values from 0 to 3, each once within a row
- diagonal: bfloat16 [128, 32, 320, 320], P('surf', 'wall'), may hold values from -1 to 8
- lifting: bfloat16 [128, 32, 6, 80, 320], P('surf', 'wall'), may hold values from -0.625 to 0.625
- inverse_rows: bfloat16 [128, 32, 80, 320], P('surf', 'wall'), may hold values from -0.25 to 0.25
Outputs:
- next_basis: bfloat16 [128, 32, 320, 256], P('surf', 'wall')
- coefs: float32 [2, 256], replicated
The draws below stay inside these ranges and needn't reach their ends.
Inputs may be any that keep to these rules, and one draw needn't show every extreme that they name: `lengths`: in every patch of 4 lines one line has 32 elements and another has 1.
All inputs are finite; a program needn't handle non-finite values.
Results may differ from the reference program's by a relative error of at most 0.00135.
Values may be sent and summed in bfloat16 or wider, within the bound.
No kernel may reach another device: no remote copies, remote signals or barrier semaphores. Data moves between devices by JAX's collectives and lax.ppermute only.
A program may use at most 64 MiB of HBM per device.

```python
import math
import jax
import jax.numpy as jnp
from jax import lax

VARS = 5
NODE1D = 4
BLOCK = 320
FACE = 80
LINES_DEV = 4
R = 256
PATCHES = 32
LINES = 128
WALLPOS = 32


def draw_vector(key, part):
    subkeys = jax.random.split(key, 2)
    line_frac = jnp.arange(LINES, dtype=jnp.float32) / max(LINES - 1, 1)
    jitter = jnp.exp(jax.random.uniform(subkeys[0], (LINES, WALLPOS), jnp.float32, 0.0, math.log(3.3)))
    element_scale = 3.0 ** (line_frac[:, None] - 0.5) * jitter / 1.8
    noise = jax.random.truncated_normal(subkeys[1], -6.0, 6.0, (LINES, WALLPOS, BLOCK, R), jnp.float32)
    return (noise * element_scale[:, :, None, None]).astype(jnp.bfloat16)


def draw_diagonal(key, part):
    subkeys = jax.random.split(key, 2)
    wall_frac = jnp.arange(WALLPOS, dtype=jnp.float32) / max(WALLPOS - 1, 1)
    line_frac = jnp.arange(LINES, dtype=jnp.float32) / max(LINES - 1, 1)
    jitter = jnp.exp(jax.random.uniform(subkeys[0], (LINES, WALLPOS), jnp.float32, 0.0, math.log(1.5)))
    shift_term = 0.25 * 5.0 ** wall_frac[None, :] * 2.0 ** line_frac[:, None] * jitter
    offdiag = jax.random.truncated_normal(subkeys[1], -6.0, 6.0, (LINES, WALLPOS, BLOCK, BLOCK), jnp.float32)
    offdiag = offdiag / math.sqrt(BLOCK)
    unit_matrix = jnp.eye(BLOCK, dtype=jnp.float32)
    return (offdiag + shift_term[:, :, None, None] * unit_matrix).astype(jnp.bfloat16)


def draw_lengths(key, part):
    subkeys = jax.random.split(key, 3)
    baseline = jax.random.randint(subkeys[0], (PATCHES, LINES_DEV), 1, WALLPOS + 1)
    longest = jax.random.randint(subkeys[1], (PATCHES, 1), 0, LINES_DEV)
    shortest = (longest + 1 + jax.random.randint(subkeys[2], (PATCHES, 1), 0, LINES_DEV - 1)) % LINES_DEV
    slots = jnp.arange(LINES_DEV)[None, :]
    baseline = jnp.where(slots == longest, WALLPOS, baseline)
    baseline = jnp.where(slots == shortest, 1, baseline)
    return baseline.reshape(LINES).astype(jnp.int32)


def steps_of(key, dims, shards, smallest, high):
    def one(axis_at, parts):
        draws = jax.random.uniform(jax.random.fold_in(jax.random.fold_in(key, 6), axis_at), (parts,), jnp.float32, smallest / len(shards), high / len(shards))
        return jnp.repeat(jnp.exp(draws), dims[axis_at] // parts).reshape((-1,) + (1,) * (len(dims) - axis_at - 1))

    gain = one(*shards[0])
    for cut in shards[1:]:
        gain = gain * one(*cut)
    return gain


def scatter_about(rng, dims, scale, reach, cuts=(), held_as=jnp.bfloat16):
    values = scale * jax.random.normal(rng, dims, jnp.float32)
    if cuts:
        values = values * steps_of(rng, dims, cuts, -0.22, 0.18)
    return jnp.clip(values, -reach, reach).astype(held_as)


def setup_inputs(seed: int = 0) -> dict:
    streams_of = jax.random.split(jax.random.key(seed), 7)
    vector = draw_vector(jax.random.fold_in(streams_of[6], 71), 0)
    lengths = draw_lengths(jax.random.fold_in(streams_of[6], 71), 0)
    north_of = jax.vmap(lambda own: jax.random.permutation(own, LINES_DEV))(jax.random.split(streams_of[2], PATCHES)).reshape((PATCHES, LINES_DEV)).astype(jnp.int32)
    diagonal = draw_diagonal(jax.random.fold_in(streams_of[6], 71), 0)
    lifting = scatter_about(streams_of[4], (LINES, WALLPOS, 6, FACE, BLOCK), FACE ** -0.5, 0.625, ((0, 32), (1, 8)))
    inverse_rows = scatter_about(streams_of[5], (LINES, WALLPOS, FACE, BLOCK), (2 * BLOCK) ** -0.5, 0.25, ((0, 32), (1, 8)))
    return {"vector": vector, "lengths": lengths, "north_of": north_of, "diagonal": diagonal, "lifting": lifting, "inverse_rows": inverse_rows}


FULL_ACCURACY = lax.Precision.HIGHEST

def face_traces(values):
    leading = values.shape[:-2]
    column_entries = values.shape[-1]
    nodal_cube = values.reshape(leading + (VARS, NODE1D, NODE1D, NODE1D, column_entries))
    last_node = NODE1D - 1

    def flatten(piece):
        return piece.reshape(leading + (FACE, column_entries))
    bottom_face = flatten(nodal_cube[..., 0, :])
    top_face = flatten(nodal_cube[..., last_node, :])
    west_face = flatten(nodal_cube[..., 0, :, :, :])
    east_face = flatten(nodal_cube[..., last_node, :, :, :])
    south_face = flatten(nodal_cube[..., 0, :, :])
    north_face = flatten(nodal_cube[..., last_node, :, :])
    return (bottom_face, top_face, west_face, east_face, south_face, north_face)

def reference(vector, lengths, north_of, diagonal, lifting, inverse_rows):
    positions = jnp.arange(WALLPOS, dtype=jnp.int32)
    living = (positions[None, :] < lengths[:, None]).astype(jnp.float32)
    masked = vector * living[:, :, None, None].astype(jnp.bfloat16)
    bottom_face, top_face, west_face, east_face, south_face, north_face = face_traces(masked)
    zero_row = jnp.zeros_like(top_face[:, :1])
    from_below = jnp.concatenate([zero_row, top_face[:, :-1]], axis=1)
    from_above = jnp.concatenate([bottom_face[:, 1:], zero_row], axis=1)
    from_west = jnp.roll(east_face, 1, axis=0)
    from_east = jnp.roll(west_face, -1, axis=0)
    patch_base = (jnp.arange(PATCHES, dtype=jnp.int32) * LINES_DEV)[:, None]
    north_line = (patch_base + north_of).reshape(LINES).astype(jnp.int32)
    south_line = jnp.zeros((LINES,), jnp.int32).at[north_line].set(jnp.arange(LINES, dtype=jnp.int32))
    from_north = south_face[north_line]
    from_south = north_face[south_line]
    neighbours = jnp.stack([from_below, from_above, from_west, from_east, from_south, from_north], axis=2)

    def per_line(pieces):
        diagonal_row_block, lifted_line_term, inverse_line, line_under_mask, adjacent_line, living_line = pieces
        matrix_product = jnp.einsum('ont,oti->oni', diagonal_row_block.astype(jnp.float32), line_under_mask.astype(jnp.float32), precision=FULL_ACCURACY)
        matrix_product = matrix_product + jnp.einsum('ovih,ovip->ohp', lifted_line_term.astype(jnp.float32), adjacent_line.astype(jnp.float32), precision=FULL_ACCURACY)
        matrix_product = matrix_product * living_line[:, None, None]

        def advance(carried, inputs):
            product_now, lower_lift, inverse_now, alive_now = inputs
            eliminated = alive_now * (product_now - jnp.dot(lower_lift.T, carried, precision=FULL_ACCURACY))
            return (jnp.dot(inverse_now, eliminated, precision=FULL_ACCURACY), eliminated)
        start = jnp.zeros((FACE, R), jnp.float32)
        _, eliminated = lax.scan(advance, start, (matrix_product, lifted_line_term[:, 0].astype(jnp.float32), inverse_line.astype(jnp.float32), living_line))
        return eliminated
    eliminated = lax.map(per_line, (diagonal, lifting, inverse_rows, masked, neighbours, living))
    masked_wide = masked.astype(jnp.float32)
    coupling_total = lax.optimization_barrier(jnp.sum(masked_wide * eliminated, axis=(0, 1, 2)))
    self_sum = lax.optimization_barrier(jnp.sum(masked_wide * masked_wide, axis=(0, 1, 2)))
    projection = coupling_total / self_sum
    remainder = eliminated - projection * masked_wide
    entries = LINES * WALLPOS * BLOCK
    spread = jnp.sqrt(lax.optimization_barrier(jnp.sum(remainder * remainder, axis=(0, 1, 2))) / entries + 1e-06)
    next_basis = (remainder / spread).astype(jnp.bfloat16)
    coefs = jnp.stack([projection, spread])
    return (next_basis, coefs)
```

```python
import functools

import jax
import jax.numpy as jnp
from jax import lax
from jax.experimental import pallas as pl
from jax.experimental.pallas import tpu as pltpu
from jax.sharding import Mesh
from jax.sharding import PartitionSpec as P

BLOCK = 320
FACE = 80
LINES_HERE = 4
SEGMENT = 4
MOVING = 3
R = 256
HALF = 128
WALL = ("y", "core")
SURF = ("x", "z")
F32 = jnp.float32
BF16 = jnp.bfloat16
EXACT = lax.Precision.HIGHEST
VMEM = pltpu.VMEM
SMEM = pltpu.SMEM

AT_WALL, AT_CORE, AT_Y, AT_ODD, AT_LENGTH, AT_NORTH = 0, 1, 2, 3, 4, 8


def in_vmem():
    return pl.BlockSpec(memory_space=VMEM)


def in_smem():
    return pl.BlockSpec(memory_space=SMEM)


def living_here(info, line):
    return jnp.clip(info[AT_LENGTH + line] - SEGMENT * info[AT_WALL], 0, SEGMENT)


def shortest_line(info):
    at = jnp.int32(3)
    for line in (2, 1, 0):
        at = jnp.where(info[AT_LENGTH + line] == 1, line, at)
    return at


def line_in_slot(slot, short):
    return jnp.where(slot == MOVING, short, slot + (slot >= short).astype(jnp.int32))


def list_living(info, listed):
    short = shortest_line(info)
    count = jnp.int32(0)
    for slot in range(LINES_HERE):
        here = living_here(info, line_in_slot(slot, short))
        for position in range(SEGMENT):
            listed[count] = slot * SEGMENT + position
            count = count + (position < here).astype(jnp.int32)
    return count


def for_living(info, listed, body, together=2):
    count = list_living(info, listed)
    short = shortest_line(info)

    @pl.loop(0, (count + together - 1) // together)
    def _(trip):
        for part in range(together):
            entry = listed[jnp.minimum(trip * together + part, count - 1)]
            slot = entry // SEGMENT
            body(slot, line_in_slot(slot, short), entry % SEGMENT)


def face_rows(first_face):
    row = lax.broadcasted_iota(jnp.int32, (2 * FACE, BLOCK), 0)
    column = lax.broadcasted_iota(jnp.int32, (2 * FACE, BLOCK), 1)
    second = (row >= FACE).astype(jnp.int32)
    entry = row - FACE * second
    if first_face == 0:
        source = 4 * entry + 3 * second
    else:
        source = 16 * (entry >> 2) + (entry & 3) + 12 * second
    return (column == source).astype(BF16)


def pick(rows, values):
    return jnp.dot(rows, values, preferred_element_type=F32).astype(BF16)


def a_face(block, end):
    return jnp.concatenate([block[64 * v + 16 * end : 64 * v + 16 * end + 16] for v in range(5)], axis=0)


def split_exactly(values):
    high = values.astype(BF16)
    low = (values - high.astype(F32)).astype(BF16)
    return high, low


def transposed_times(left, right):
    return lax.dot_general(left, right, (((0,), (0,)), ((), ())), preferred_element_type=F32)


def mapped(matrix, state):
    return jnp.dot(matrix, state, precision=EXACT, preferred_element_type=F32)


def edges_kernel(info, vector, over_core, over_y, over_pair, over_next):
    core, odd = info[AT_CORE], info[AT_ODD]
    short = shortest_line(info)
    rows = face_rows(0)
    zero = jnp.zeros((FACE, R), BF16)
    for slot in range(MOVING):
        line = line_in_slot(slot, short)
        here = living_here(info, line)
        down = jnp.where(here > 0, pick(rows[:FACE], vector[line, 0]), zero)
        up = jnp.where(here > SEGMENT - 1, pick(rows[FACE:], vector[line, SEGMENT - 1]), zero)
        over_core[slot] = jnp.where(core == 0, up, down)
        over_y[slot] = jnp.where(core == 0, down, up)
    first, last = living_here(info, 0), living_here(info, LINES_HERE - 1)
    for position in range(SEGMENT):
        west = jnp.where(position < first, a_face(vector[0, position], 0), zero)
        east = jnp.where(position < last, a_face(vector[LINES_HERE - 1, position], 3), zero)
        over_pair[position] = jnp.where(odd == 0, east, west)
        over_next[position] = jnp.where(odd == 0, west, east)


def maps_kernel(info, lifting_below, inverse, steps, prefixes, whole):
    short = shortest_line(info)
    for slot in range(MOVING):
        line = line_in_slot(slot, short)
        here = living_here(info, line)
        so_far = None
        for position in range(SEGMENT):
            step = lax.dot_general(
                inverse[line, position],
                lifting_below[line, position, 0],
                (((1,), (1,)), ((), ())),
                preferred_element_type=F32,
            )
            step = jnp.where(position < here, -step, 0.0)
            steps[slot, position] = step
            so_far = step if position == 0 else jnp.dot(step, so_far, precision=EXACT, preferred_element_type=F32)
            prefixes[slot, position] = so_far
        whole[slot] = jnp.concatenate([so_far, jnp.zeros((FACE, HALF - FACE), F32)], axis=1)


def diagonal_kernel(info, vector, diagonal, map_here, map_beside, product, traces, chip_map, listed):
    core = info[AT_CORE]
    for slot in range(MOVING):
        first = jnp.where(core == 0, map_here[slot], map_beside[slot])
        second = jnp.where(core == 0, map_beside[slot], map_here[slot])
        chip_map[slot] = mapped(second[:, :FACE], first)
    wall_rows, b_rows = face_rows(0), face_rows(4)
    for line in range(LINES_HERE):
        here = living_here(info, line)
        for position in range(SEGMENT):

            @pl.when(position >= here)
            def _():
                traces[line, position] = jnp.zeros((6, FACE, R), BF16)

    def body(slot, line, position):
        values = vector[line, position]
        product[line, position] = jnp.dot(diagonal[line, position], values, preferred_element_type=F32)
        wall_faces = pick(wall_rows, values)
        b_faces = pick(b_rows, values)
        traces[line, position, 0] = wall_faces[:FACE]
        traces[line, position, 1] = wall_faces[FACE:]
        traces[line, position, 2] = a_face(values, 0)
        traces[line, position, 3] = a_face(values, 3)
        traces[line, position, 4] = b_faces[:FACE]
        traces[line, position, 5] = b_faces[FACE:]

    for_living(info, listed, body)


def product_kernel(
    info,
    traces,
    over_core,
    over_y,
    over_pair,
    over_next,
    lifting,
    inverse,
    steps,
    product_in,
    product,
    carries,
    outgoing,
    listed,
    driven,
):
    core, odd = info[AT_CORE], info[AT_ODD]
    short = shortest_line(info)
    driven[...] = jnp.zeros_like(driven)
    zero = jnp.zeros((FACE, R), BF16)

    def body(slot, line, position):
        wall_slot = jnp.minimum(slot, MOVING - 1)
        moving = slot < MOVING
        from_core = jnp.where(moving, over_core[wall_slot], zero)
        from_y = jnp.where(moving, over_y[wall_slot], zero)
        below_edge = jnp.where(core == 0, from_y, from_core)
        above_edge = jnp.where(core == 0, from_core, from_y)
        below = jnp.where(position == 0, below_edge, traces[line, jnp.maximum(position - 1, 0), 1])
        above = jnp.where(
            position == SEGMENT - 1, above_edge, traces[line, jnp.minimum(position + 1, SEGMENT - 1), 0]
        )
        west_edge = jnp.where(odd == 0, over_next[position], over_pair[position])
        east_edge = jnp.where(odd == 0, over_pair[position], over_next[position])
        west = jnp.where(line == 0, west_edge, traces[jnp.maximum(line - 1, 0), position, 3])
        east = jnp.where(
            line == LINES_HERE - 1, east_edge, traces[jnp.minimum(line + 1, LINES_HERE - 1), position, 2]
        )
        north_line = info[AT_NORTH + line]
        south_line = jnp.int32(0)
        for other in range(1, LINES_HERE):
            south_line = jnp.where(info[AT_NORTH + other] == line, other, south_line)
        south = traces[south_line, position, 5]
        north = traces[north_line, position, 4]
        neighbours = jnp.concatenate([below, above, west, east, south, north], axis=0)
        blocks = lifting[line, position].reshape(6 * FACE, BLOCK)
        total = product_in[line, position] + transposed_times(blocks, neighbours)
        product[line, position] = total
        high, low = split_exactly(total)
        here = jnp.dot(inverse[line, position], jnp.concatenate([high, low], axis=1), preferred_element_type=F32)
        driven[slot, position] = here[:, :R] + here[:, R:]

    for_living(info, listed, body)
    for slot in range(MOVING):
        carried = driven[slot, 0]
        for position in range(1, SEGMENT):
            carries[slot, position - 1] = carried
            carried = driven[slot, position] + jnp.dot(
                steps[slot, position], carried, precision=EXACT, preferred_element_type=F32
            )
        outgoing[slot] = carried


def chip_kernel(info, mine, other, map_here, map_beside, chip):
    core = info[AT_CORE]
    for slot in range(MOVING):
        own, away = mine[slot], other[slot]
        first_value = jnp.where(core == 0, own[:, :HALF], away[:, HALF:])
        second_value = jnp.where(core == 0, away[:, :HALF], own[:, HALF:])
        second_map = jnp.where(core == 0, map_beside[slot], map_here[slot])
        chip[slot] = mapped(second_map[:, :FACE], first_value) + second_value


def arriving_kernel(info, one, two, three, nearest_map, next_map, arriving):
    for slot in range(MOVING):
        value = two[slot] + mapped(next_map[slot][:, :FACE], three[slot])
        arriving[slot] = one[slot] + mapped(nearest_map[slot][:, :FACE], value)


def eliminate_kernel(
    info,
    vector,
    product,
    lifting_below,
    prefixes,
    map_beside,
    carries,
    mine,
    other,
    below_out,
    eliminated,
    tiles,
    listed,
    entering,
):
    core = info[AT_CORE]
    short = shortest_line(info)
    entering[...] = jnp.zeros_like(entering)
    for slot in range(MOVING):
        left = jnp.where(core == 0, mine[slot], other[slot])
        right = jnp.where(core == 0, other[slot], mine[slot])
        value = jnp.concatenate([left, right], axis=1)
        passed = mapped(map_beside[slot][:, :FACE], value) + below_out[slot]
        value = jnp.where(core == 0, value, passed)
        entering[slot, 0] = value
        stacked = prefixes[slot].reshape(SEGMENT * FACE, FACE)[: (SEGMENT - 1) * FACE]
        moved = mapped(stacked, value)
        for position in range(1, SEGMENT):
            entering[slot, position] = carries[slot, position - 1] + moved[(position - 1) * FACE : position * FACE]

    count = list_living(info, listed)
    nothing = jnp.zeros((8, R), F32)

    def of(trip):
        entry = listed[trip]
        slot = entry // SEGMENT
        return slot, line_in_slot(slot, short), entry % SEGMENT

    def partial(values):
        return values.reshape(BLOCK // 8, 8, R).sum(axis=0)

    def correct(slot, line, position):
        high, low = split_exactly(entering[slot, position])
        block = lifting_below[line, position, 0]
        correction = transposed_times(jnp.concatenate([block, block], axis=0), jnp.concatenate([high, low], axis=0))
        eliminated[line, position] = product[line, position] - correction

    for_living(info, listed, correct)

    def products(trip, sums):
        _, line, position = of(trip)
        masked, value = vector[line, position].astype(F32), eliminated[line, position]
        return sums[0] + partial(masked * value), sums[1] + partial(masked * masked)

    cross, square = lax.fori_loop(0, count, products, (nothing, nothing))
    cross = cross.sum(axis=0, keepdims=True)
    square = square.sum(axis=0, keepdims=True)
    share = jnp.where(square > 0, cross / square, 0.0)

    def left_over(trip, total):
        _, line, position = of(trip)
        rest = eliminated[line, position] - share * vector[line, position].astype(F32)
        return total + partial(rest * rest)

    rest = lax.fori_loop(0, count, left_over, nothing).sum(axis=0, keepdims=True)
    pieces = [part[:, at : at + HALF] for part in (cross, square, rest) for at in (0, HALF)]
    tile = jnp.concatenate(pieces + [jnp.zeros((2, HALF), F32)], axis=0)
    for copy in range(tiles.shape[0]):
        tiles[copy] = tile


def merged(tiles):
    cross, square, rest = tiles[:, 0:2], tiles[:, 2:4], tiles[:, 4:6]
    all_cross, all_square = cross.sum(axis=0), square.sum(axis=0)
    own = jnp.where(square > 0, cross / square, 0.0)
    ratio = all_cross / all_square
    away = jnp.where(square > 0, own - ratio[None], 0.0)
    all_rest = (rest + (square * away) * away).sum(axis=0)
    return all_cross, all_square, all_rest, ratio


def merge_kernel(tiles_in, tiles):
    cross, square, rest, _ = merged(tiles_in[...])
    tile = jnp.concatenate([cross, square, rest, jnp.zeros((2, HALF), F32)], axis=0)
    for copy in range(tiles.shape[0]):
        tiles[copy] = tile


def finish_kernel(entries, info, tiles, vector, eliminated, basis, coefs, held, sems):
    _, _, rest, ratio = merged(tiles[...])
    spread = jnp.sqrt(rest / entries + 1e-06)
    ratio = jnp.concatenate([ratio[0:1], ratio[1:2]], axis=1)
    spread = jnp.concatenate([spread[0:1], spread[1:2]], axis=1)
    coefs[...] = jnp.concatenate([ratio, spread], axis=0)
    scale = 1.0 / spread
    copies = []
    for line in range(LINES_HERE):
        here = living_here(info, line)

        @pl.loop(0, here)
        def _(position):
            masked = vector[line, position].astype(F32)
            held[line, position] = ((eliminated[line, position] - ratio * masked) * scale).astype(BF16)

        @pl.loop(here, SEGMENT)
        def _(position):
            held[line, position] = jnp.zeros((BLOCK, R), BF16)

        copy = pltpu.make_async_copy(held.at[line], basis.at[line], sems.at[line])
        copy.start()
        copies.append(copy)
    for copy in copies:
        copy.wait()


def call(kernel, outs, ins, scratch=(), limit=12, flops=0, moved=0, out_specs=None):
    return pl.pallas_call(
        kernel,
        out_shape=outs,
        in_specs=[in_smem() if arg.dtype == jnp.int32 else in_vmem() for arg in ins],
        out_specs=out_specs or jax.tree.map(lambda _: in_vmem(), outs),
        scratch_shapes=list(scratch),
        compiler_params=pltpu.CompilerParams(vmem_limit_bytes=limit * 2**20),
        cost_estimate=pl.CostEstimate(flops=flops, bytes_accessed=moved, transcendentals=0),
        name=getattr(kernel, "__name__", "finish_kernel"),
    )(*ins)


def shaped(*shape, dtype=F32):
    return jax.ShapeDtypeStruct(shape, dtype)


LISTED = pltpu.SMEM((LINES_HERE * SEGMENT + 1,), jnp.int32)


def per_device(vector, lengths, north_of, diagonal, lifting, inverse_rows):
    wall, core, y = lax.axis_index(WALL), lax.axis_index("core"), lax.axis_index("y")
    odd = lax.axis_index("z") % 2
    info = jnp.concatenate([jnp.stack([wall, core, y, odd]).astype(jnp.int32), lengths, north_of[0]])
    edge = shaped(MOVING, FACE, R, dtype=BF16)
    side = shaped(SEGMENT, FACE, R, dtype=BF16)
    over_core, over_y, over_pair, over_next = call(edges_kernel, (edge, edge, side, side), (info, vector))
    walls, surfs = lax.axis_size(WALL), lax.axis_size(SURF)
    swap = [(0, 1), (1, 0)]
    over_core = lax.ppermute(over_core, "core", swap)
    rungs = [(i, i + 1) for i in range(1, walls - 1, 2)]
    over_y = lax.ppermute(over_y, WALL, rungs + [(b, a) for a, b in rungs])
    over_pair = lax.ppermute(over_pair, SURF, [(i, i ^ 1) for i in range(surfs)])
    nexts = [(i, (i + 1) % surfs) for i in range(1, surfs, 2)]
    over_next = lax.ppermute(over_next, SURF, nexts + [(b, a) for a, b in nexts])

    lower = lifting[:, :, 0:1]
    steps, prefixes, whole = call(
        maps_kernel,
        (shaped(MOVING, SEGMENT, FACE, FACE), shaped(MOVING, SEGMENT, FACE, FACE), shaped(MOVING, FACE, HALF)),
        (info, lower, inverse_rows),
        flops=10**8,
        moved=2 * 10**6,
    )
    map_beside = lax.ppermute(whole, "core", swap)
    product, traces, chip_map = call(
        diagonal_kernel,
        (
            shaped(LINES_HERE, SEGMENT, BLOCK, R),
            shaped(LINES_HERE, SEGMENT, 6, FACE, R, dtype=BF16),
            shaped(MOVING, FACE, HALF),
        ),
        (info, vector, diagonal, whole, map_beside),
        (LISTED,),
        flops=2 * 10**9,
        moved=14 * 10**6,
    )
    ranks = lax.axis_size("y")

    def up_chips(value, far):
        return lax.ppermute(value, "y", [(i, i + far) for i in range(ranks - far)])

    maps_below = [up_chips(chip_map, far) for far in (1, 2)]
    product, carries, outgoing = call(
        product_kernel,
        (
            shaped(LINES_HERE, SEGMENT, BLOCK, R),
            shaped(MOVING, SEGMENT - 1, FACE, R),
            shaped(MOVING, FACE, R),
        ),
        (info, traces, over_core, over_y, over_pair, over_next, lifting, inverse_rows, steps, product),
        (LISTED, pltpu.VMEM((LINES_HERE, SEGMENT, FACE, R), F32)),
        flops=2 * 10**9,
        moved=20 * 10**6,
    )
    beside = lax.ppermute(outgoing, "core", swap)
    chip = call(chip_kernel, shaped(MOVING, FACE, HALF), (info, outgoing, beside, whole, map_beside), flops=10**7)
    from_chips = [up_chips(chip, far) for far in range(1, ranks)]
    arriving = call(arriving_kernel, shaped(MOVING, FACE, HALF), (info, *from_chips, *maps_below), flops=10**7)
    arriving_beside = lax.ppermute(arriving, "core", swap)
    eliminated, tiles = call(
        eliminate_kernel,
        (shaped(LINES_HERE, SEGMENT, BLOCK, R), shaped(surfs, 8, HALF)),
        (info, vector, product, lower, prefixes, map_beside, carries, arriving, arriving_beside, beside),
        (LISTED, pltpu.VMEM((LINES_HERE, SEGMENT, FACE, R), F32)),
        flops=10**9,
        moved=10**7,
    )
    tiles = lax.all_to_all(tiles, SURF, 0, 0, tiled=True)
    tiles = call(merge_kernel, shaped(walls, 8, HALF), (tiles,))
    tiles = lax.all_to_all(tiles, WALL, 0, 0, tiled=True)
    entries = LINES_HERE * SEGMENT * BLOCK * walls * surfs
    return call(
        functools.partial(finish_kernel, entries),
        (shaped(LINES_HERE, SEGMENT, BLOCK, R, dtype=BF16), shaped(2, R)),
        (info, tiles, vector, eliminated),
        (pltpu.VMEM((LINES_HERE, SEGMENT, BLOCK, R), BF16), pltpu.SemaphoreType.DMA((LINES_HERE,))),
        out_specs=(pl.BlockSpec(memory_space=pl.ANY), in_vmem()),
    )


def solution(mesh):
    split = Mesh(mesh.devices.reshape(4, 2, 4, 8), ("y", "core", "x", "z"))
    placed = (
        P(SURF, WALL, None, None),
        P(SURF),
        P(SURF, None),
        P(SURF, WALL, None, None),
        P(SURF, WALL, None, None, None),
        P(SURF, WALL, None, None),
    )
    return jax.shard_map(
        per_device,
        mesh=split,
        in_specs=placed,
        out_specs=(P(SURF, WALL, None, None), P()),
        check_vma=False,
    )
```

```python
import functools

import jax
import jax.numpy as jnp
from jax import lax
from jax.experimental import pallas as pl
from jax.experimental.pallas import tpu as pltpu
from jax.sharding import Mesh
from jax.sharding import PartitionSpec as P

BLOCK = 320
FACE = 80
LINES_HERE = 4
SEGMENT = 4
MOVING = 3
R = 256
ELEMENTS = LINES_HERE * SEGMENT
HALF = 128
OWN_MAP = slice(R, R + 80)
Y_MAP = slice(R + HALF, R + HALF + 80)
WALL = ("y", "core")
SURF = ("x", "z")
F32 = jnp.float32
BF16 = jnp.bfloat16
EXACT = lax.Precision.HIGHEST
VMEM = pltpu.VMEM
SMEM = pltpu.SMEM


def in_vmem():
    return pl.BlockSpec(memory_space=VMEM)


def in_smem():
    return pl.BlockSpec(memory_space=SMEM)


def wall_here():
    return lax.axis_index("y") * 2 + lax.axis_index("core")


def living_here(lengths, line):
    return jnp.clip(lengths[line] - SEGMENT * wall_here(), 0, SEGMENT)


def shortest_line(lengths):
    at = jnp.int32(3)
    for line in (2, 1, 0):
        at = jnp.where(lengths[line] == 1, line, at)
    return at


def line_in_slot(slot, short):
    return jnp.where(slot == MOVING, short, slot + (slot >= short).astype(jnp.int32))


def list_living(lengths, listed, slots=LINES_HERE, rest_behind=False):
    short = shortest_line(lengths)
    count = jnp.int32(0)
    for slot in range(slots):
        here = living_here(lengths, line_in_slot(slot, short))
        for position in range(SEGMENT):
            entry = slot * SEGMENT + position
            alive = (position < here).astype(jnp.int32)
            listed[count if not rest_behind else jnp.where(alive == 1, count, ELEMENTS - 1 - (entry - count))] = entry
            count = count + alive
    return count


def for_listed(lengths, listed, count, body, together=4, after=None):
    short = shortest_line(lengths)

    @pl.loop(0, (count + together - 1) // together)
    def _(trip):
        for part in range(together):
            entry = listed[jnp.minimum(trip * together + part, count - 1)]
            slot = entry // SEGMENT
            body(slot, line_in_slot(slot, short), entry % SEGMENT)
        if after is not None:
            for part in range(together):
                after(trip * together + part)


def wall_face_rows():
    row = lax.broadcasted_iota(jnp.int32, (2 * FACE, BLOCK), 0)
    column = lax.broadcasted_iota(jnp.int32, (2 * FACE, BLOCK), 1)
    second = (row >= FACE).astype(jnp.int32)
    return (column == 4 * (row - FACE * second) + 3 * second).astype(BF16)


def pick(rows, values):
    return jnp.dot(rows, values, preferred_element_type=F32).astype(BF16)


def a_face(block, end):
    return jnp.concatenate([block[64 * v + 16 * end : 64 * v + 16 * end + 16] for v in range(5)], axis=0)


def split_exactly(values):
    high = values.astype(BF16)
    low = (values - high.astype(F32)).astype(BF16)
    return high, low


def transposed_times(left, right):
    return lax.dot_general(left, right, (((0,), (0,)), ((), ())), preferred_element_type=F32)


def mapped(matrix, state):
    matrix_high, matrix_low = split_exactly(matrix)
    high, low = split_exactly(state)
    rows = matrix.shape[0]
    both = jnp.dot(jnp.concatenate([matrix_high, matrix_low], axis=0), high, preferred_element_type=F32)
    return both[:rows] + (both[rows:] + jnp.dot(matrix_high, low, preferred_element_type=F32))


def edges_kernel(
    lengths_hbm, vector, over_core, over_y, over_pair, over_next, lengths, ends, west, east, sems, run_sems
):
    core, odd = lax.axis_index("core"), lax.axis_index("z") % 2
    copies = [pltpu.make_async_copy(lengths_hbm, lengths, sems.at[0])]
    for end, position in enumerate((0, SEGMENT - 1)):
        copies.append(pltpu.make_async_copy(vector.at[:, position], ends.at[end], sems.at[1 + end]))
    for at, (line, first_row, face) in enumerate(((0, 0, west), (LINES_HERE - 1, 48, east))):
        for run in range(5):
            source = vector.at[line, :, pl.ds(64 * run + first_row, 16)]
            target = face.at[:, pl.ds(16 * run, 16)]
            copies.append(pltpu.make_async_copy(source, target, run_sems.at[at, run]))
    for copy in copies:
        copy.start()
    rows = wall_face_rows()
    for copy in copies:
        copy.wait()
    short = shortest_line(lengths)
    zero = jnp.zeros((FACE, R), BF16)
    for slot in range(MOVING):
        line = line_in_slot(slot, short)
        here = living_here(lengths, line)
        down = jnp.where(here > 0, pick(rows[:FACE], ends[0, line]), zero)
        up = jnp.where(here > SEGMENT - 1, pick(rows[FACE:], ends[1, line]), zero)
        over_core[slot] = jnp.where(core == 0, up, down)
        over_y[slot] = jnp.where(core == 0, down, up)
    first, last = living_here(lengths, 0), living_here(lengths, LINES_HERE - 1)
    for position in range(SEGMENT):
        from_first = jnp.where(position < first, west[position], zero)
        from_last = jnp.where(position < last, east[position], zero)
        over_pair[position] = jnp.where(odd == 0, from_last, from_first)
        over_next[position] = jnp.where(odd == 0, from_first, from_last)


def maps_kernel(
    lengths_hbm,
    after,
    lifting_hbm,
    inverse_hbm,
    diagonal_hbm,
    steps,
    prefixes,
    whole,
    lower,
    inverse,
    diagonal,
    lengths,
    sems,
    lengths_sem,
):
    needed = [pltpu.make_async_copy(lengths_hbm, lengths, lengths_sem)]
    for line in range(LINES_HERE):
        needed.append(pltpu.make_async_copy(inverse_hbm.at[line], inverse.at[line], sems.at[0, line]))
        needed.append(pltpu.make_async_copy(lifting_hbm.at[line, :, 0], lower.at[line], sems.at[1, line]))
    later = [
        pltpu.make_async_copy(diagonal_hbm.at[line], diagonal.at[line], sems.at[2, line]) for line in range(LINES_HERE)
    ]
    for copy in needed + later:
        copy.start()
    for copy in needed:
        copy.wait()
    short = shortest_line(lengths)
    lines = [line_in_slot(slot, short) for slot in range(MOVING)]
    so_far = [None] * MOVING
    for position in range(SEGMENT):
        for slot, line in enumerate(lines):
            step = lax.dot_general(
                inverse[line, position],
                lower[line, position],
                (((1,), (1,)), ((), ())),
                preferred_element_type=F32,
            )
            steps[slot, position] = jnp.where(position < living_here(lengths, line), -step, 0.0)
    for position in range(SEGMENT):
        for slot in range(MOVING):
            step = steps[slot, position]
            so_far[slot] = step if position == 0 else mapped(step, so_far[slot])
            if position < SEGMENT - 1:
                prefixes[slot, position] = so_far[slot]
    for slot in range(MOVING):
        whole[slot] = jnp.concatenate([so_far[slot], jnp.zeros((FACE, HALF - FACE), F32)], axis=1)
    for copy in later:
        copy.wait()


def diagonal_kernel(lengths, vector, diagonal, lifting_hbm, product, traces, lifting, listed, wide, sems):
    copies = [
        pltpu.make_async_copy(lifting_hbm.at[line, :, pl.ds(1, 5)], lifting.at[line], sems.at[line])
        for line in range(LINES_HERE)
    ]
    for copy in copies:
        copy.start()
    for line in range(LINES_HERE):
        here = living_here(lengths, line)
        for position in range(SEGMENT):

            @pl.when(position >= here)
            def _():
                traces[line, position] = jnp.zeros((6, FACE, R), BF16)

    def body(slot, line, position):
        values = vector[line, position]
        product[line, position] = jnp.dot(diagonal[line, position], values, preferred_element_type=F32)
        whole = values.astype(F32)
        for half in range(2):
            columns = slice(half * HALF, (half + 1) * HALF)
            wide[half] = whole[:, columns]
            for face, first in ((0, 0), (1, 3)):
                traces[line, position, face, :, columns] = wide[half, pl.ds(first, FACE, stride=4), :].astype(BF16)
        traces[line, position, 2] = a_face(values, 0)
        traces[line, position, 3] = a_face(values, 3)
        runs = whole.reshape(10, 4, 8, R)
        upper = lax.broadcasted_iota(jnp.int32, (10, 8, R), 1) < 4
        south = jnp.where(upper, runs[:, 0], pltpu.roll(runs[:, 2], 4, axis=1))
        north = jnp.where(upper, pltpu.roll(runs[:, 1], 4, axis=1), runs[:, 3])
        traces[line, position, 4] = south.reshape(FACE, R).astype(BF16)
        traces[line, position, 5] = north.reshape(FACE, R).astype(BF16)

    for_listed(lengths, listed, list_living(lengths, listed), body)
    for copy in copies:
        copy.wait()


def product_kernel(
    lengths,
    norths,
    traces,
    over_core,
    over_y,
    over_pair,
    over_next,
    lower,
    lifting,
    inverse,
    steps,
    map_here,
    map_y,
    product_in,
    product,
    carries,
    outgoing,
    listed,
    driven,
):
    core, odd = lax.axis_index("core"), lax.axis_index("z") % 2
    zero = jnp.zeros((FACE, R), BF16)

    def multiply(slot, line, position):
        wall_slot = jnp.minimum(slot, MOVING - 1)
        moving = slot < MOVING
        from_core = jnp.where(moving, over_core[wall_slot], zero)
        from_y = jnp.where(moving, over_y[wall_slot], zero)
        below_edge = jnp.where(core == 0, from_y, from_core)
        above_edge = jnp.where(core == 0, from_core, from_y)
        below = jnp.where(position == 0, below_edge, traces[line, jnp.maximum(position - 1, 0), 1])
        above = jnp.where(
            position == SEGMENT - 1, above_edge, traces[line, jnp.minimum(position + 1, SEGMENT - 1), 0]
        )
        west_edge = jnp.where(odd == 0, over_next[position], over_pair[position])
        east_edge = jnp.where(odd == 0, over_pair[position], over_next[position])
        west = jnp.where(line == 0, west_edge, traces[jnp.maximum(line - 1, 0), position, 3])
        east = jnp.where(
            line == LINES_HERE - 1, east_edge, traces[jnp.minimum(line + 1, LINES_HERE - 1), position, 2]
        )
        north_line = norths[0, line]
        south_line = jnp.int32(0)
        for other in range(1, LINES_HERE):
            south_line = jnp.where(norths[0, other] == line, other, south_line)
        south = traces[south_line, position, 5]
        north = traces[north_line, position, 4]
        neighbours = jnp.concatenate([below, above, west, east, south, north], axis=0)
        upper_blocks = lifting[line, position].reshape(5 * FACE, BLOCK)
        blocks = jnp.concatenate([lower[line, position], upper_blocks], axis=0)
        product[line, position] = product_in[line, position] + transposed_times(blocks, neighbours)

    count = list_living(lengths, listed)
    for_listed(lengths, listed, count, multiply)

    for slot in range(MOVING):
        for position in range(SEGMENT):

            @pl.when(position >= living_here(lengths, line_in_slot(slot, shortest_line(lengths))))
            def _():
                driven[slot, position] = jnp.zeros((FACE, R), F32)

    def drive(slot, line, position):
        high, low = split_exactly(product[line, position])
        rows = inverse[line, position]
        tail = rows[:, 256:]
        driven[slot, position] = jnp.dot(
            jnp.concatenate([rows[:, :256], rows[:, :256], tail, tail], axis=1),
            jnp.concatenate([high[:256], low[:256], high[256:], low[256:]], axis=0),
            preferred_element_type=F32,
        )

    for_listed(lengths, listed, list_living(lengths, listed, MOVING), drive)
    carried = [driven[slot, 0] for slot in range(MOVING)]
    for position in range(1, SEGMENT):
        for slot in range(MOVING):
            carries[slot, position - 1] = carried[slot]
            carried[slot] = driven[slot, position] + mapped(steps[slot, position], carried[slot])
    for slot in range(MOVING):
        outgoing[slot] = jnp.concatenate([carried[slot], map_here[slot], map_y[slot]], axis=1)


def chip_kernel(mine, other, near, far):
    core, y = lax.axis_index("core"), lax.axis_index("y")
    values = []
    for slot in range(MOVING):
        own, away = mine[slot], other[slot]
        first_value = jnp.where(core == 0, own[:, :HALF], away[:, HALF:R])
        second_value = jnp.where(core == 0, away[:, :HALF], own[:, HALF:R])
        second_map = jnp.where(core == 0, away[:, OWN_MAP], own[:, OWN_MAP])
        values.append(mapped(second_map, first_value) + second_value)
    for slot in range(MOVING):
        near[slot] = values[slot]
        far[slot] = values[slot]

    @pl.when(y == 0)
    def _():
        through_chip(mine, other, values, far)


def through_chip(mine, other, values, results):
    core = lax.axis_index("core")
    moved = []
    for slot, value in enumerate(values):
        own, away = mine[slot][:, Y_MAP], other[slot][:, Y_MAP]
        moved.append(mapped(jnp.where(core == 0, own, away), value))
    for slot, value in enumerate(moved):
        own, away = mine[slot][:, Y_MAP], other[slot][:, Y_MAP]
        results[slot] = mapped(jnp.where(core == 0, away, own), value)


def arriving_kernel(one, two, three, mine, other, arriving):
    y = lax.axis_index("y")
    below = [two[slot] + three[slot] for slot in range(MOVING)]
    for slot in range(MOVING):
        arriving[slot] = below[slot]

    @pl.when(y == 3)
    def _():
        through_chip(mine, other, below, arriving)

    for slot in range(MOVING):
        arriving[slot] = arriving[slot] + one[slot]


def eliminate_kernel(
    lengths,
    vector,
    product,
    lower,
    prefixes,
    carries,
    mine,
    other,
    beside,
    eliminated,
    tiles,
    listed,
    entering,
):
    core = lax.axis_index("core")
    short = shortest_line(lengths)
    entering[...] = jnp.zeros_like(entering)
    values = []
    for slot in range(MOVING):
        left = jnp.where(core == 0, mine[slot], other[slot])
        right = jnp.where(core == 0, other[slot], mine[slot])
        value = jnp.concatenate([left, right], axis=1)
        passed = mapped(beside[slot][:, OWN_MAP], value) + beside[slot][:, :R]
        values.append(jnp.where(core == 0, value, passed))
    for slot, value in enumerate(values):
        entering[slot, 0] = value
        moved = mapped(prefixes[slot].reshape((SEGMENT - 1) * FACE, FACE), value)
        for position in range(1, SEGMENT):
            entering[slot, position] = carries[slot, position - 1] + moved[(position - 1) * FACE : position * FACE]

    count = list_living(lengths, listed)
    nothing = jnp.zeros((8, R), F32)

    def of(trip):
        entry = listed[trip]
        slot = entry // SEGMENT
        return slot, line_in_slot(slot, short), entry % SEGMENT

    def partial(values):
        return values.reshape(BLOCK // 8, 8, R).sum(axis=0)

    def correct(slot, line, position):
        high, low = split_exactly(entering[slot, position])
        block = lower[line, position]
        correction = transposed_times(jnp.concatenate([block, block], axis=0), jnp.concatenate([high, low], axis=0))
        eliminated[line, position] = product[line, position] - correction

    for_listed(lengths, listed, count, correct)

    def products(trip, sums):
        _, line, position = of(trip)
        masked, value = vector[line, position].astype(F32), eliminated[line, position]
        return sums[0] + partial(masked * value), sums[1] + partial(masked * masked)

    cross, square = lax.fori_loop(0, count, products, (nothing, nothing))
    cross = cross.sum(axis=0, keepdims=True)
    square = square.sum(axis=0, keepdims=True)
    share = jnp.where(square > 0, cross / square, 0.0)

    def left_over(trip, total):
        _, line, position = of(trip)
        rest = eliminated[line, position] - share * vector[line, position].astype(F32)
        return total + partial(rest * rest)

    rest = lax.fori_loop(0, count, left_over, nothing).sum(axis=0, keepdims=True)
    pieces = [part[:, at : at + HALF] for part in (cross, square, rest) for at in (0, HALF)]
    tile = jnp.concatenate(pieces + [jnp.zeros((2, HALF), F32)], axis=0)
    for copy in range(tiles.shape[0]):
        tiles[copy] = tile


def merged(tiles):
    cross, square, rest = tiles[:, 0:2], tiles[:, 2:4], tiles[:, 4:6]
    all_cross, all_square = cross.sum(axis=0), square.sum(axis=0)
    own = jnp.where(square > 0, cross / square, 0.0)
    ratio = all_cross / all_square
    away = jnp.where(square > 0, own - ratio[None], 0.0)
    all_rest = (rest + (square * away) * away).sum(axis=0)
    return all_cross, all_square, all_rest, ratio


def merge_kernel(tiles_in, tiles):
    cross, square, rest, _ = merged(tiles_in[...])
    tile = jnp.concatenate([cross, square, rest, jnp.zeros((2, HALF), F32)], axis=0)
    for copy in range(tiles.shape[0]):
        tiles[copy] = tile


def finish_kernel(entries, lengths, tiles, vector, eliminated, basis, coefs, listed, held, sems):
    _, _, rest, ratio = merged(tiles[...])
    spread = jnp.sqrt(rest / entries + 1e-06)
    ratio = jnp.concatenate([ratio[0:1], ratio[1:2]], axis=1)
    spread = jnp.concatenate([spread[0:1], spread[1:2]], axis=1)
    coefs[...] = jnp.concatenate([ratio, spread], axis=0)
    scale = 1.0 / spread
    short = shortest_line(lengths)
    count = list_living(lengths, listed, rest_behind=True)

    def copy_of(trip):
        line, position = line_in_slot(listed[trip] // SEGMENT, short), listed[trip] % SEGMENT
        return pltpu.make_async_copy(held.at[line, position], basis.at[line, position], sems.at[trip])

    @pl.loop(count, ELEMENTS)
    def _(trip):
        line, position = line_in_slot(listed[trip] // SEGMENT, short), listed[trip] % SEGMENT
        held[line, position] = jnp.zeros((BLOCK, R), BF16)
        copy_of(trip).start()

    def body(slot, line, position):
        masked = vector[line, position].astype(F32)
        held[line, position] = ((eliminated[line, position] - ratio * masked) * scale).astype(BF16)

    def after(trip):
        @pl.when(trip < count)
        def _():
            copy_of(trip).start()

    for_listed(lengths, listed, count, body, 2, after)

    @pl.loop(0, ELEMENTS)
    def _(trip):
        copy_of(trip).wait()


def call(kernel, outs, ins, scratch=(), limit=12, flops=0, moved=0, out_specs=None, in_hbm=()):
    return pl.pallas_call(
        kernel,
        out_shape=outs,
        in_specs=[
            pl.BlockSpec(memory_space=pltpu.HBM) if at in in_hbm else in_smem() if arg.dtype == jnp.int32 else in_vmem()
            for at, arg in enumerate(ins)
        ],
        out_specs=out_specs or jax.tree.map(lambda _: in_vmem(), outs),
        scratch_shapes=list(scratch),
        compiler_params=pltpu.CompilerParams(vmem_limit_bytes=limit * 2**20),
        cost_estimate=pl.CostEstimate(flops=flops, bytes_accessed=moved, transcendentals=0),
        name=getattr(kernel, "__name__", "finish_kernel"),
    )(*[pltpu.with_memory_space_constraint(arg, pltpu.HBM) if at in in_hbm else arg for at, arg in enumerate(ins)])


def shaped(*shape, dtype=F32):
    return jax.ShapeDtypeStruct(shape, dtype)


LISTED = pltpu.SMEM((LINES_HERE * SEGMENT + 1,), jnp.int32)


def per_device(vector, lengths, north_of, diagonal, lifting, inverse_rows):
    edge = shaped(MOVING, FACE, R, dtype=BF16)
    side = shaped(SEGMENT, FACE, R, dtype=BF16)
    over_core, over_y, over_pair, over_next = call(
        edges_kernel,
        (edge, edge, side, side),
        (lengths, vector),
        (
            pltpu.SMEM((LINES_HERE,), jnp.int32),
            pltpu.VMEM((2, LINES_HERE, BLOCK, R), BF16),
            pltpu.VMEM((SEGMENT, FACE, R), BF16),
            pltpu.VMEM((SEGMENT, FACE, R), BF16),
            pltpu.SemaphoreType.DMA((3,)),
            pltpu.SemaphoreType.DMA((2, 5)),
        ),
        in_hbm=(0, 1),
    )
    walls, surfs = lax.axis_size(WALL), lax.axis_size(SURF)
    swap = [(0, 1), (1, 0)]
    first_edge = over_core
    over_core = lax.ppermute(over_core, "core", swap)
    rungs = [(i, i + 1) for i in range(1, walls - 1, 2)]
    over_y = lax.ppermute(over_y, WALL, rungs + [(b, a) for a, b in rungs])
    over_pair = lax.ppermute(over_pair, SURF, [(i, i ^ 1) for i in range(surfs)])
    nexts = [(i, (i + 1) % surfs) for i in range(1, surfs, 2)]
    over_next = lax.ppermute(over_next, SURF, nexts + [(b, a) for a, b in nexts])

    blocks = shaped(LINES_HERE, SEGMENT, FACE, BLOCK, dtype=BF16)
    steps, prefixes, whole, lower, inverse, diagonal_here = call(
        maps_kernel,
        (
            shaped(MOVING, SEGMENT, FACE, FACE),
            shaped(MOVING, SEGMENT - 1, FACE, FACE),
            shaped(MOVING, FACE, HALF),
            blocks,
            blocks,
            shaped(LINES_HERE, SEGMENT, BLOCK, BLOCK, dtype=BF16),
        ),
        (lengths, first_edge, lifting, inverse_rows, diagonal),
        (pltpu.SMEM((LINES_HERE,), jnp.int32), pltpu.SemaphoreType.DMA((3, LINES_HERE)), pltpu.SemaphoreType.DMA),
        in_hbm=(0, 2, 3, 4),
    )
    map_y = lax.ppermute(whole, "y", [(1, 0), (2, 3)])
    product, traces, lifting_here = call(
        diagonal_kernel,
        (
            shaped(LINES_HERE, SEGMENT, BLOCK, R),
            shaped(LINES_HERE, SEGMENT, 6, FACE, R, dtype=BF16),
            shaped(LINES_HERE, SEGMENT, 5, FACE, BLOCK, dtype=BF16),
        ),
        (lengths, vector, diagonal_here, lifting),
        (LISTED, pltpu.VMEM((2, BLOCK, HALF), F32), pltpu.SemaphoreType.DMA((LINES_HERE,))),
        in_hbm=(3,),
    )
    product, carries, outgoing = call(
        product_kernel,
        (
            shaped(LINES_HERE, SEGMENT, BLOCK, R),
            shaped(MOVING, SEGMENT - 1, FACE, R),
            shaped(MOVING, FACE, R + 2 * HALF),
        ),
        (
            lengths,
            north_of,
            traces,
            over_core,
            over_y,
            over_pair,
            over_next,
            lower,
            lifting_here,
            inverse,
            steps,
            whole,
            map_y,
            product,
        ),
        (LISTED, pltpu.VMEM((LINES_HERE, SEGMENT, FACE, R), F32)),
    )
    ranks = lax.axis_size("y")

    def up_chips(value, far):
        return lax.ppermute(value, "y", [(i, i + far) for i in range(ranks - far)])

    beside = lax.ppermute(outgoing, "core", swap)
    near, far = call(chip_kernel, (shaped(MOVING, FACE, HALF), shaped(MOVING, FACE, HALF)), (outgoing, beside))
    one, two, three = up_chips(near, 1), up_chips(far, 2), up_chips(far, 3)
    arriving = call(arriving_kernel, shaped(MOVING, FACE, HALF), (one, two, three, outgoing, beside))
    arriving_beside = lax.ppermute(arriving, "core", swap)
    eliminated, tiles = call(
        eliminate_kernel,
        (shaped(LINES_HERE, SEGMENT, BLOCK, R), shaped(surfs, 8, HALF)),
        (lengths, vector, product, lower, prefixes, carries, arriving, arriving_beside, beside),
        (LISTED, pltpu.VMEM((LINES_HERE, SEGMENT, FACE, R), F32)),
        flops=10**9,
        moved=10**7,
    )
    tiles = lax.all_to_all(tiles, SURF, 0, 0, tiled=True)
    tiles = call(merge_kernel, shaped(walls, 8, HALF), (tiles,))
    tiles = lax.all_to_all(tiles, WALL, 0, 0, tiled=True)
    entries = LINES_HERE * SEGMENT * BLOCK * walls * surfs
    return call(
        functools.partial(finish_kernel, entries),
        (shaped(LINES_HERE, SEGMENT, BLOCK, R, dtype=BF16), shaped(2, R)),
        (lengths, tiles, vector, eliminated),
        (LISTED, pltpu.VMEM((LINES_HERE, SEGMENT, BLOCK, R), BF16), pltpu.SemaphoreType.DMA((ELEMENTS,))),
        out_specs=(pl.BlockSpec(memory_space=pl.ANY), in_vmem()),
    )


def solution(mesh):
    split = Mesh(mesh.devices.reshape(4, 2, 4, 8), ("y", "core", "x", "z"))
    placed = (
        P(SURF, WALL, None, None),
        P(SURF),
        P(SURF, None),
        P(SURF, WALL, None, None),
        P(SURF, WALL, None, None, None),
        P(SURF, WALL, None, None),
    )
    return jax.shard_map(
        per_device,
        mesh=split,
        in_specs=placed,
        out_specs=(P(SURF, WALL, None, None), P()),
        check_vma=False,
    )
```

```python
import functools

import jax
import jax.numpy as jnp
from jax import lax
from jax.experimental import pallas as pl
from jax.experimental.pallas import tpu as pltpu
from jax.sharding import Mesh
from jax.sharding import PartitionSpec as P

BLOCK = 320
FACE = 80
LINES_HERE = 4
SEGMENT = 4
MOVING = 3
R = 256
ELEMENTS = LINES_HERE * SEGMENT
HALF = 128
OWN_MAPS, Y_MAPS = MOVING, MOVING + 1
WALL = ("y", "core")
SURF = ("x", "z")
F32 = jnp.float32
BF16 = jnp.bfloat16
EXACT = lax.Precision.HIGHEST
VMEM = pltpu.VMEM
SMEM = pltpu.SMEM


def in_vmem():
    return pl.BlockSpec(memory_space=VMEM)


def in_smem():
    return pl.BlockSpec(memory_space=SMEM)


def wall_here():
    return lax.axis_index("y") * 2 + lax.axis_index("core")


def living_here(lengths, line):
    return jnp.clip(lengths[line] - SEGMENT * wall_here(), 0, SEGMENT)


def shortest_line(lengths):
    at = jnp.int32(3)
    for line in (2, 1, 0):
        at = jnp.where(lengths[line] == 1, line, at)
    return at


def line_in_slot(slot, short):
    return jnp.where(slot == MOVING, short, slot + (slot >= short).astype(jnp.int32))


def list_living(lengths, listed, slots=LINES_HERE, rest_behind=False):
    short = shortest_line(lengths)
    count = jnp.int32(0)
    for slot in range(slots):
        here = living_here(lengths, line_in_slot(slot, short))
        for position in range(SEGMENT):
            entry = slot * SEGMENT + position
            alive = (position < here).astype(jnp.int32)
            listed[count if not rest_behind else jnp.where(alive == 1, count, ELEMENTS - 1 - (entry - count))] = entry
            count = count + alive
    return count


def for_listed(lengths, listed, count, body, together=4, after=None):
    short = shortest_line(lengths)

    def one(trip):
        entry = listed[trip]
        slot = entry // SEGMENT
        body(slot, line_in_slot(slot, short), entry % SEGMENT)

    def group(first, size):
        for part in range(size):
            one(first + part)
        if after is not None:
            for part in range(size):
                after(first + part)

    whole = count // together

    @pl.loop(0, whole)
    def _(trip):
        group(trip * together, together)

    @pl.loop(whole * together, count)
    def _(trip):
        group(trip, 1)


def wall_face_rows():
    row = lax.broadcasted_iota(jnp.int32, (2 * FACE, BLOCK), 0)
    column = lax.broadcasted_iota(jnp.int32, (2 * FACE, BLOCK), 1)
    second = (row >= FACE).astype(jnp.int32)
    return (column == 4 * (row - FACE * second) + 3 * second).astype(BF16)


def pick(rows, values):
    return jnp.dot(rows, values, preferred_element_type=F32).astype(BF16)


def a_face(block, end):
    return jnp.concatenate([block[64 * v + 16 * end : 64 * v + 16 * end + 16] for v in range(5)], axis=0)


def partial(values):
    return values.reshape(BLOCK // 8, 8, R).sum(axis=0)


def split_exactly(values):
    high = values.astype(BF16)
    low = (values - high.astype(F32)).astype(BF16)
    return high, low


def transposed_times(left, right):
    return lax.dot_general(left, right, (((0,), (0,)), ((), ())), preferred_element_type=F32)


def mapped(matrix, state):
    matrix_high, matrix_low = split_exactly(matrix)
    high, low = split_exactly(state)
    rows = matrix.shape[0]
    both = jnp.dot(jnp.concatenate([matrix_high, matrix_low], axis=0), high, preferred_element_type=F32)
    return both[:rows] + (both[rows:] + jnp.dot(matrix_high, low, preferred_element_type=F32))


def edges_kernel(
    lengths_hbm,
    vector,
    lifting_hbm,
    inverse_hbm,
    diagonal_hbm,
    over_core,
    over_y,
    over_pair,
    over_next,
    steps,
    prefixes,
    whole,
    lower,
    inverse,
    diagonal,
    lengths,
    ends,
    west,
    east,
    sems,
    run_sems,
    block_sems,
):
    core, odd = lax.axis_index("core"), lax.axis_index("z") % 2
    copies = [pltpu.make_async_copy(lengths_hbm, lengths, sems.at[0])]
    for end, position in enumerate((0, SEGMENT - 1)):
        copies.append(pltpu.make_async_copy(vector.at[:, position], ends.at[end], sems.at[1 + end]))
    for at, (line, first_row, face) in enumerate(((0, 0, west), (LINES_HERE - 1, 48, east))):
        for run in range(5):
            source = vector.at[line, :, pl.ds(64 * run + first_row, 16)]
            target = face.at[:, pl.ds(16 * run, 16)]
            copies.append(pltpu.make_async_copy(source, target, run_sems.at[at, run]))
    needed = []
    for line in range(LINES_HERE):
        needed.append(pltpu.make_async_copy(inverse_hbm.at[line], inverse.at[line], block_sems.at[0, line]))
        needed.append(pltpu.make_async_copy(lifting_hbm.at[line, :, 0], lower.at[line], block_sems.at[1, line]))
    later = [
        pltpu.make_async_copy(diagonal_hbm.at[line], diagonal.at[line], block_sems.at[2, line])
        for line in range(LINES_HERE)
    ]
    for copy in copies + needed + later:
        copy.start()
    rows = wall_face_rows()
    for copy in copies:
        copy.wait()
    short = shortest_line(lengths)
    zero = jnp.zeros((FACE, R), BF16)
    for slot in range(MOVING):
        line = line_in_slot(slot, short)
        here = living_here(lengths, line)
        down = jnp.where(here > 0, pick(rows[:FACE], ends[0, line]), zero)
        up = jnp.where(here > SEGMENT - 1, pick(rows[FACE:], ends[1, line]), zero)
        over_core[slot] = jnp.where(core == 0, up, down)
        over_y[slot] = jnp.where(core == 0, down, up)
    first, last = living_here(lengths, 0), living_here(lengths, LINES_HERE - 1)
    for position in range(SEGMENT):
        from_first = jnp.where(position < first, west[position], zero)
        from_last = jnp.where(position < last, east[position], zero)
        over_pair[position] = jnp.where(odd == 0, from_last, from_first)
        over_next[position] = jnp.where(odd == 0, from_first, from_last)
    for copy in needed:
        copy.wait()
    lines = [line_in_slot(slot, short) for slot in range(MOVING)]
    so_far = [None] * MOVING
    for position in range(SEGMENT):
        for slot, line in enumerate(lines):
            step = lax.dot_general(
                inverse[line, position],
                lower[line, position],
                (((1,), (1,)), ((), ())),
                preferred_element_type=F32,
            )
            steps[slot, position] = jnp.where(position < living_here(lengths, line), -step, 0.0)
    for position in range(SEGMENT):
        for slot in range(MOVING):
            step = steps[slot, position]
            so_far[slot] = step if position == 0 else mapped(step, so_far[slot])
            if position < SEGMENT - 1:
                prefixes[slot, position] = so_far[slot]
    whole[...] = jnp.concatenate(so_far + [jnp.zeros((FACE, R - MOVING * FACE), F32)], axis=1)
    for copy in later:
        copy.wait()


def diagonal_kernel(lengths, vector, diagonal, lifting_hbm, product, traces, lifting, squares, listed, wide, sems):
    copies = [
        pltpu.make_async_copy(lifting_hbm.at[line, :, pl.ds(1, 5)], lifting.at[line], sems.at[line])
        for line in range(LINES_HERE)
    ]
    for copy in copies:
        copy.start()
    for line in range(LINES_HERE):
        here = living_here(lengths, line)
        for position in range(SEGMENT):

            @pl.when(position >= here)
            def _():
                traces[line, position] = jnp.zeros((6, FACE, R), BF16)

    squares[...] = jnp.zeros_like(squares)

    def body(slot, line, position):
        values = vector[line, position]
        product[line, position] = jnp.dot(diagonal[line, position], values, preferred_element_type=F32)
        whole = values.astype(F32)
        squares[...] += partial(whole * whole)
        for half in range(2):
            columns = slice(half * HALF, (half + 1) * HALF)
            wide[half] = whole[:, columns]
            for face, first in ((0, 0), (1, 3)):
                traces[line, position, face, :, columns] = wide[half, pl.ds(first, FACE, stride=4), :].astype(BF16)
        traces[line, position, 2] = a_face(values, 0)
        traces[line, position, 3] = a_face(values, 3)
        runs = whole.reshape(10, 4, 8, R)
        upper = lax.broadcasted_iota(jnp.int32, (10, 8, R), 1) < 4
        south = jnp.where(upper, runs[:, 0], pltpu.roll(runs[:, 2], 4, axis=1))
        north = jnp.where(upper, pltpu.roll(runs[:, 1], 4, axis=1), runs[:, 3])
        traces[line, position, 4] = south.reshape(FACE, R).astype(BF16)
        traces[line, position, 5] = north.reshape(FACE, R).astype(BF16)

    for_listed(lengths, listed, list_living(lengths, listed), body)
    for copy in copies:
        copy.wait()


def product_kernel(
    lengths,
    norths,
    traces,
    over_core,
    over_y,
    over_pair,
    over_next,
    lower,
    lifting,
    inverse,
    steps,
    map_here,
    map_y,
    product_in,
    product,
    carries,
    outgoing,
    listed,
    driven,
):
    core, odd = lax.axis_index("core"), lax.axis_index("z") % 2
    zero = jnp.zeros((FACE, R), BF16)

    def multiply(slot, line, position):
        wall_slot = jnp.minimum(slot, MOVING - 1)
        moving = slot < MOVING
        from_core = jnp.where(moving, over_core[wall_slot], zero)
        from_y = jnp.where(moving, over_y[wall_slot], zero)
        below_edge = jnp.where(core == 0, from_y, from_core)
        above_edge = jnp.where(core == 0, from_core, from_y)
        below = jnp.where(position == 0, below_edge, traces[line, jnp.maximum(position - 1, 0), 1])
        above = jnp.where(
            position == SEGMENT - 1, above_edge, traces[line, jnp.minimum(position + 1, SEGMENT - 1), 0]
        )
        west_edge = jnp.where(odd == 0, over_next[position], over_pair[position])
        east_edge = jnp.where(odd == 0, over_pair[position], over_next[position])
        west = jnp.where(line == 0, west_edge, traces[jnp.maximum(line - 1, 0), position, 3])
        east = jnp.where(
            line == LINES_HERE - 1, east_edge, traces[jnp.minimum(line + 1, LINES_HERE - 1), position, 2]
        )
        north_line = norths[0, line]
        south_line = jnp.int32(0)
        for other in range(1, LINES_HERE):
            south_line = jnp.where(norths[0, other] == line, other, south_line)
        south = traces[south_line, position, 5]
        north = traces[north_line, position, 4]
        neighbours = jnp.concatenate([below, above, west, east, south, north], axis=0)
        upper_blocks = lifting[line, position].reshape(5 * FACE, BLOCK)
        blocks = jnp.concatenate([lower[line, position], upper_blocks], axis=0)
        product[line, position] = product_in[line, position] + transposed_times(blocks, neighbours)

    count = list_living(lengths, listed)
    for_listed(lengths, listed, count, multiply)

    for slot in range(MOVING):
        for position in range(SEGMENT):

            @pl.when(position >= living_here(lengths, line_in_slot(slot, shortest_line(lengths))))
            def _():
                driven[slot, position] = jnp.zeros((FACE, R), F32)

    def drive(slot, line, position):
        high, low = split_exactly(product[line, position])
        rows = inverse[line, position]
        tail = rows[:, 256:]
        driven[slot, position] = jnp.dot(
            jnp.concatenate([rows[:, :256], rows[:, :256], tail, tail], axis=1),
            jnp.concatenate([high[:256], low[:256], high[256:], low[256:]], axis=0),
            preferred_element_type=F32,
        )

    for_listed(lengths, listed, list_living(lengths, listed, MOVING), drive)
    carried = [driven[slot, 0] for slot in range(MOVING)]
    for position in range(1, SEGMENT):
        for slot in range(MOVING):
            carries[slot, position - 1] = carried[slot]
            carried[slot] = driven[slot, position] + mapped(steps[slot, position], carried[slot])
    for slot in range(MOVING):
        outgoing[slot] = carried[slot]
    outgoing[OWN_MAPS] = map_here[...]
    outgoing[Y_MAPS] = map_y[...]


def map_of(maps, slot):
    return maps[:, slot * FACE : (slot + 1) * FACE]


def chip_kernel(mine, other, near, far):
    core, y = lax.axis_index("core"), lax.axis_index("y")
    second_maps = jnp.where(core == 0, other[OWN_MAPS], mine[OWN_MAPS])
    values = []
    for slot in range(MOVING):
        own, away = mine[slot], other[slot]
        first_value = jnp.where(core == 0, own[:, :HALF], away[:, HALF:])
        second_value = jnp.where(core == 0, away[:, :HALF], own[:, HALF:])
        values.append(mapped(map_of(second_maps, slot), first_value) + second_value)
    for slot in range(MOVING):
        near[slot] = values[slot]
        far[slot] = values[slot]

    @pl.when(y == 0)
    def _():
        through_chip(mine, other, values, far)


def through_chip(mine, other, values, results):
    core = lax.axis_index("core")
    first_maps = jnp.where(core == 0, mine[Y_MAPS], other[Y_MAPS])
    second_maps = jnp.where(core == 0, other[Y_MAPS], mine[Y_MAPS])
    moved = [mapped(map_of(first_maps, slot), value) for slot, value in enumerate(values)]
    for slot, value in enumerate(moved):
        results[slot] = mapped(map_of(second_maps, slot), value)


def arriving_kernel(one, two, three, mine, other, arriving):
    y = lax.axis_index("y")
    below = [two[slot] + three[slot] for slot in range(MOVING)]
    for slot in range(MOVING):
        arriving[slot] = below[slot]

    @pl.when(y == 3)
    def _():
        through_chip(mine, other, below, arriving)

    for slot in range(MOVING):
        arriving[slot] = arriving[slot] + one[slot]


def eliminate_kernel(
    lengths,
    vector,
    squares,
    product,
    lower,
    prefixes,
    carries,
    mine,
    other,
    beside,
    eliminated,
    tiles,
    listed,
    entering,
    sums,
):
    core = lax.axis_index("core")
    short = shortest_line(lengths)
    entering[...] = jnp.zeros_like(entering)
    values = []
    for slot in range(MOVING):
        left = jnp.where(core == 0, mine[slot], other[slot])
        right = jnp.where(core == 0, other[slot], mine[slot])
        value = jnp.concatenate([left, right], axis=1)
        passed = mapped(map_of(beside[OWN_MAPS], slot), value) + beside[slot]
        values.append(jnp.where(core == 0, value, passed))
    for slot, value in enumerate(values):
        entering[slot, 0] = value
        moved = mapped(prefixes[slot].reshape((SEGMENT - 1) * FACE, FACE), value)
        for position in range(1, SEGMENT):
            entering[slot, position] = carries[slot, position - 1] + moved[(position - 1) * FACE : position * FACE]

    count = list_living(lengths, listed)
    sums[...] = jnp.zeros_like(sums)

    def correct(slot, line, position):
        high, low = split_exactly(entering[slot, position])
        block = lower[line, position]
        correction = transposed_times(jnp.concatenate([block, block], axis=0), jnp.concatenate([high, low], axis=0))
        value = product[line, position] - correction
        eliminated[line, position] = value
        masked = vector[line, position].astype(F32)
        sums[0] += partial(masked * value)

    for_listed(lengths, listed, count, correct)
    cross = sums[0].sum(axis=0, keepdims=True)
    square = squares[...].sum(axis=0, keepdims=True)
    share = jnp.where(square > 0, cross / square, 0.0)

    def leave(slot, line, position):
        rest = eliminated[line, position] - share * vector[line, position].astype(F32)
        sums[1] += partial(rest * rest)

    for_listed(lengths, listed, count, leave)
    rest = sums[1].sum(axis=0, keepdims=True)
    pieces = [part[:, at : at + HALF] for part in (cross, square, rest) for at in (0, HALF)]
    tile = jnp.concatenate(pieces + [jnp.zeros((2, HALF), F32)], axis=0)
    for copy in range(tiles.shape[0]):
        tiles[copy] = tile


def merged(tiles):
    cross, square, rest = tiles[:, 0:2], tiles[:, 2:4], tiles[:, 4:6]
    all_cross, all_square = cross.sum(axis=0), square.sum(axis=0)
    own = jnp.where(square > 0, cross / square, 0.0)
    ratio = all_cross / all_square
    away = jnp.where(square > 0, own - ratio[None], 0.0)
    all_rest = (rest + (square * away) * away).sum(axis=0)
    return all_cross, all_square, all_rest, ratio


def merge_kernel(tiles_in, tiles):
    cross, square, rest, _ = merged(tiles_in[...])
    tile = jnp.concatenate([cross, square, rest, jnp.zeros((2, HALF), F32)], axis=0)
    for copy in range(tiles.shape[0]):
        tiles[copy] = tile


def finish_kernel(entries, lengths, tiles, vector, eliminated, basis, coefs, listed, held, sems):
    _, _, rest, ratio = merged(tiles[...])
    spread = jnp.sqrt(rest / entries + 1e-06)
    ratio = jnp.concatenate([ratio[0:1], ratio[1:2]], axis=1)
    spread = jnp.concatenate([spread[0:1], spread[1:2]], axis=1)
    coefs[...] = jnp.concatenate([ratio, spread], axis=0)
    scale = 1.0 / spread
    short = shortest_line(lengths)
    count = list_living(lengths, listed, rest_behind=True)

    def copy_of(trip):
        line, position = line_in_slot(listed[trip] // SEGMENT, short), listed[trip] % SEGMENT
        return pltpu.make_async_copy(held.at[line, position], basis.at[line, position], sems.at[trip])

    @pl.loop(count, ELEMENTS)
    def _(trip):
        line, position = line_in_slot(listed[trip] // SEGMENT, short), listed[trip] % SEGMENT
        held[line, position] = jnp.zeros((BLOCK, R), BF16)
        copy_of(trip).start()

    def body(slot, line, position):
        masked = vector[line, position].astype(F32)
        held[line, position] = ((eliminated[line, position] - ratio * masked) * scale).astype(BF16)

    def after(trip):
        copy_of(trip).start()

    for_listed(lengths, listed, count, body, 4, after)

    @pl.loop(0, ELEMENTS)
    def _(trip):
        copy_of(trip).wait()


def call(kernel, outs, ins, scratch=(), limit=12, flops=0, moved=0, out_specs=None, in_hbm=()):
    return pl.pallas_call(
        kernel,
        out_shape=outs,
        in_specs=[
            pl.BlockSpec(memory_space=pltpu.HBM) if at in in_hbm else in_smem() if arg.dtype == jnp.int32 else in_vmem()
            for at, arg in enumerate(ins)
        ],
        out_specs=out_specs or jax.tree.map(lambda _: in_vmem(), outs),
        scratch_shapes=list(scratch),
        compiler_params=pltpu.CompilerParams(vmem_limit_bytes=limit * 2**20),
        cost_estimate=pl.CostEstimate(flops=flops, bytes_accessed=moved, transcendentals=0),
        name=getattr(kernel, "__name__", "finish_kernel"),
    )(*[pltpu.with_memory_space_constraint(arg, pltpu.HBM) if at in in_hbm else arg for at, arg in enumerate(ins)])


def shaped(*shape, dtype=F32):
    return jax.ShapeDtypeStruct(shape, dtype)


LISTED = pltpu.SMEM((LINES_HERE * SEGMENT + 1,), jnp.int32)


def per_device(vector, lengths, north_of, diagonal, lifting, inverse_rows):
    edge = shaped(MOVING, FACE, R, dtype=BF16)
    side = shaped(SEGMENT, FACE, R, dtype=BF16)
    blocks = shaped(LINES_HERE, SEGMENT, FACE, BLOCK, dtype=BF16)
    over_core, over_y, over_pair, over_next, steps, prefixes, whole, lower, inverse, diagonal_here = call(
        edges_kernel,
        (
            edge,
            edge,
            side,
            side,
            shaped(MOVING, SEGMENT, FACE, FACE),
            shaped(MOVING, SEGMENT - 1, FACE, FACE),
            shaped(FACE, R),
            blocks,
            blocks,
            shaped(LINES_HERE, SEGMENT, BLOCK, BLOCK, dtype=BF16),
        ),
        (lengths, vector, lifting, inverse_rows, diagonal),
        (
            pltpu.SMEM((LINES_HERE,), jnp.int32),
            pltpu.VMEM((2, LINES_HERE, BLOCK, R), BF16),
            pltpu.VMEM((SEGMENT, FACE, R), BF16),
            pltpu.VMEM((SEGMENT, FACE, R), BF16),
            pltpu.SemaphoreType.DMA((3,)),
            pltpu.SemaphoreType.DMA((2, 5)),
            pltpu.SemaphoreType.DMA((3, LINES_HERE)),
        ),
        in_hbm=(0, 1, 2, 3, 4),
    )
    walls, surfs = lax.axis_size(WALL), lax.axis_size(SURF)
    swap = [(0, 1), (1, 0)]
    over_core = lax.ppermute(over_core, "core", swap)
    rungs = [(i, i + 1) for i in range(1, walls - 1, 2)]
    over_y = lax.ppermute(over_y, WALL, rungs + [(b, a) for a, b in rungs])
    over_pair = lax.ppermute(over_pair, SURF, [(i, i ^ 1) for i in range(surfs)])
    nexts = [(i, (i + 1) % surfs) for i in range(1, surfs, 2)]
    over_next = lax.ppermute(over_next, SURF, nexts + [(b, a) for a, b in nexts])

    map_y = lax.ppermute(whole, "y", [(1, 0), (2, 3)])
    product, traces, lifting_here, squares = call(
        diagonal_kernel,
        (
            shaped(LINES_HERE, SEGMENT, BLOCK, R),
            shaped(LINES_HERE, SEGMENT, 6, FACE, R, dtype=BF16),
            shaped(LINES_HERE, SEGMENT, 5, FACE, BLOCK, dtype=BF16),
            shaped(8, R),
        ),
        (lengths, vector, diagonal_here, lifting),
        (LISTED, pltpu.VMEM((2, BLOCK, HALF), F32), pltpu.SemaphoreType.DMA((LINES_HERE,))),
        in_hbm=(3,),
    )
    product, carries, outgoing = call(
        product_kernel,
        (
            shaped(LINES_HERE, SEGMENT, BLOCK, R),
            shaped(MOVING, SEGMENT - 1, FACE, R),
            shaped(MOVING + 2, FACE, R),
        ),
        (
            lengths,
            north_of,
            traces,
            over_core,
            over_y,
            over_pair,
            over_next,
            lower,
            lifting_here,
            inverse,
            steps,
            whole,
            map_y,
            product,
        ),
        (LISTED, pltpu.VMEM((LINES_HERE, SEGMENT, FACE, R), F32)),
    )
    ranks = lax.axis_size("y")

    def up_chips(value, far):
        return lax.ppermute(value, "y", [(i, i + far) for i in range(ranks - far)])

    beside = lax.ppermute(outgoing, "core", swap)
    near, far = call(chip_kernel, (shaped(MOVING, FACE, HALF), shaped(MOVING, FACE, HALF)), (outgoing, beside))
    one, two, three = up_chips(near, 1), up_chips(far, 2), up_chips(far, 3)
    arriving = call(arriving_kernel, shaped(MOVING, FACE, HALF), (one, two, three, outgoing, beside))
    arriving_beside = lax.ppermute(arriving, "core", swap)
    eliminated, tiles = call(
        eliminate_kernel,
        (shaped(LINES_HERE, SEGMENT, BLOCK, R), shaped(surfs, 8, HALF)),
        (lengths, vector, squares, product, lower, prefixes, carries, arriving, arriving_beside, beside),
        (LISTED, pltpu.VMEM((LINES_HERE, SEGMENT, FACE, R), F32), pltpu.VMEM((2, 8, R), F32)),
        flops=10**9,
        moved=10**7,
    )
    tiles = lax.all_to_all(tiles, SURF, 0, 0, tiled=True)
    tiles = call(merge_kernel, shaped(walls, 8, HALF), (tiles,))
    tiles = lax.all_to_all(tiles, WALL, 0, 0, tiled=True)
    entries = LINES_HERE * SEGMENT * BLOCK * walls * surfs
    return call(
        functools.partial(finish_kernel, entries),
        (shaped(LINES_HERE, SEGMENT, BLOCK, R, dtype=BF16), shaped(2, R)),
        (lengths, tiles, vector, eliminated),
        (LISTED, pltpu.VMEM((LINES_HERE, SEGMENT, BLOCK, R), BF16), pltpu.SemaphoreType.DMA((ELEMENTS,))),
        out_specs=(pl.BlockSpec(memory_space=pl.ANY), in_vmem()),
    )


def solution(mesh):
    split = Mesh(mesh.devices.reshape(4, 2, 4, 8), ("y", "core", "x", "z"))
    placed = (
        P(SURF, WALL, None, None),
        P(SURF),
        P(SURF, None),
        P(SURF, WALL, None, None),
        P(SURF, WALL, None, None, None),
        P(SURF, WALL, None, None),
    )
    return jax.shard_map(
        per_device,
        mesh=split,
        in_specs=placed,
        out_specs=(P(SURF, WALL, None, None), P()),
        check_vma=False,
    )
```

```python
import functools

import jax
import jax.numpy as jnp
from jax import lax
from jax.experimental import pallas as pl
from jax.experimental.pallas import tpu as pltpu
from jax.sharding import Mesh
from jax.sharding import PartitionSpec as P

BLOCK = 320
FACE = 80
LINES_HERE = 4
SEGMENT = 4
MOVING = 3
R = 256
HALF = 128
OWN_MAPS, Y_MAPS = MOVING, MOVING + 1
WALL = ("y", "core")
SURF = ("x", "z")
F32 = jnp.float32
BF16 = jnp.bfloat16
EXACT = lax.Precision.HIGHEST
VMEM = pltpu.VMEM


def in_vmem():
    return pl.BlockSpec(memory_space=VMEM)


class Digits:
    def __init__(self, number, bits):
        self.number, self.bits = number, bits

    def __getitem__(self, at):
        return (self.number >> (self.bits * at)) & ((1 << self.bits) - 1)


def lengths_and_norths(tile):
    return Digits(jnp.max(tile[0:8]).astype(jnp.int32), 6), Digits(jnp.max(tile[8:16]).astype(jnp.int32), 2)


def wall_here():
    return lax.axis_index("y") * 2 + lax.axis_index("core")


def living_here(lengths, line):
    return jnp.clip(lengths[line] - SEGMENT * wall_here(), 0, SEGMENT)


def shortest_line(lengths):
    at = jnp.int32(3)
    for line in (2, 1, 0):
        at = jnp.where(lengths[line] == 1, line, at)
    return at


def line_in_slot(slot, short):
    return jnp.where(slot == MOVING, short, slot + (slot >= short).astype(jnp.int32))


def list_living(lengths, listed, slots=LINES_HERE):
    short = shortest_line(lengths)
    count = jnp.int32(0)
    for slot in range(slots):
        here = living_here(lengths, line_in_slot(slot, short))
        for position in range(SEGMENT):
            listed[count] = slot * SEGMENT + position
            count = count + (position < here).astype(jnp.int32)
    return count


def for_listed(lengths, listed, count, body, together=4):
    short = shortest_line(lengths)

    def one(trip):
        entry = listed[trip]
        slot = entry // SEGMENT
        body(slot, line_in_slot(slot, short), entry % SEGMENT)

    def group(first, size):
        for part in range(size):
            one(first + part)

    whole = count // together

    @pl.loop(0, whole)
    def _(trip):
        group(trip * together, together)

    @pl.loop(whole * together, count)
    def _(trip):
        group(trip, 1)


def wall_face_rows():
    row = lax.broadcasted_iota(jnp.int32, (2 * FACE, BLOCK), 0)
    column = lax.broadcasted_iota(jnp.int32, (2 * FACE, BLOCK), 1)
    second = (row >= FACE).astype(jnp.int32)
    return (column == 4 * (row - FACE * second) + 3 * second).astype(BF16)


def pick(rows, values):
    return jnp.dot(rows, values, preferred_element_type=F32).astype(BF16)


def a_face(block, end):
    return jnp.concatenate([block[64 * v + 16 * end : 64 * v + 16 * end + 16] for v in range(5)], axis=0)


def partial(values):
    return values.reshape(BLOCK // 8, 8, R).sum(axis=0)


def split_exactly(values):
    high = values.astype(BF16)
    low = (values - high.astype(F32)).astype(BF16)
    return high, low


def transposed_times(left, right):
    return lax.dot_general(left, right, (((0,), (0,)), ((), ())), preferred_element_type=F32)


def mapped(matrix, state):
    matrix_high, matrix_low = split_exactly(matrix)
    high, low = split_exactly(state)
    rows = matrix.shape[0]
    both = jnp.dot(jnp.concatenate([matrix_high, matrix_low], axis=0), high, preferred_element_type=F32)
    return both[:rows] + (both[rows:] + jnp.dot(matrix_high, low, preferred_element_type=F32))


def edges_kernel(
    lengths_hbm,
    norths_hbm,
    vector_hbm,
    lifting_hbm,
    inverse_hbm,
    over_core,
    over_y,
    over_pair,
    over_next,
    steps,
    prefixes,
    whole,
    lower,
    inverse,
    vector,
    tile,
    lengths,
    norths,
    sems,
    block_sems,
):
    core, odd = lax.axis_index("core"), lax.axis_index("z") % 2
    copies = [
        pltpu.make_async_copy(lengths_hbm, lengths, sems.at[0]),
        pltpu.make_async_copy(norths_hbm, norths, sems.at[1]),
    ]
    for line in range(LINES_HERE):
        copies.append(pltpu.make_async_copy(vector_hbm.at[line], vector.at[line], block_sems.at[2, line]))
    needed = []
    for line in range(LINES_HERE):
        needed.append(pltpu.make_async_copy(inverse_hbm.at[line], inverse.at[line], block_sems.at[0, line]))
        needed.append(pltpu.make_async_copy(lifting_hbm.at[line, :, 0], lower.at[line], block_sems.at[1, line]))
    for copy in copies + needed:
        copy.start()
    rows = wall_face_rows()
    for copy in copies:
        copy.wait()
    length_digits, north_digits = jnp.int32(0), jnp.int32(0)
    for line in range(LINES_HERE):
        length_digits = length_digits + (lengths[line] << (6 * line))
        north_digits = north_digits + (norths[0, line] << (2 * line))
    tile[0:8] = jnp.full((8, HALF), length_digits.astype(F32))
    tile[8:16] = jnp.full((8, HALF), north_digits.astype(F32))
    short = shortest_line(lengths)
    zero = jnp.zeros((FACE, R), BF16)
    for slot in range(MOVING):
        line = line_in_slot(slot, short)
        here = living_here(lengths, line)
        down = jnp.where(here > 0, pick(rows[:FACE], vector[line, 0]), zero)
        up = jnp.where(here > SEGMENT - 1, pick(rows[FACE:], vector[line, SEGMENT - 1]), zero)
        over_core[slot] = jnp.where(core == 0, up, down)
        over_y[slot] = jnp.where(core == 0, down, up)
    first, last = living_here(lengths, 0), living_here(lengths, LINES_HERE - 1)
    for position in range(SEGMENT):
        from_first = jnp.where(position < first, a_face(vector[0, position], 0), zero)
        from_last = jnp.where(position < last, a_face(vector[LINES_HERE - 1, position], 3), zero)
        over_pair[position] = jnp.where(odd == 0, from_last, from_first)
        over_next[position] = jnp.where(odd == 0, from_first, from_last)
    for copy in needed:
        copy.wait()
    lines = [line_in_slot(slot, short) for slot in range(MOVING)]
    so_far = [None] * MOVING
    for position in range(SEGMENT):
        for slot, line in enumerate(lines):
            step = lax.dot_general(
                inverse[line, position],
                lower[line, position],
                (((1,), (1,)), ((), ())),
                preferred_element_type=F32,
            )
            steps[slot, position] = jnp.where(position < living_here(lengths, line), -step, 0.0)
    for position in range(SEGMENT):
        for slot in range(MOVING):
            step = steps[slot, position]
            so_far[slot] = step if position == 0 else mapped(step, so_far[slot])
            if position < SEGMENT - 1:
                prefixes[slot, position] = so_far[slot]
    whole[...] = jnp.concatenate(so_far + [jnp.zeros((FACE, R - MOVING * FACE), F32)], axis=1)


def diagonal_kernel(tile, vector, diagonal, lifting_hbm, product, traces, lifting, squares, listed, wide, sems):
    lengths, _ = lengths_and_norths(tile)
    copies = [
        pltpu.make_async_copy(lifting_hbm.at[line, :, pl.ds(1, 5)], lifting.at[line], sems.at[line])
        for line in range(LINES_HERE)
    ]
    for copy in copies:
        copy.start()
    for line in range(LINES_HERE):
        here = living_here(lengths, line)
        for position in range(SEGMENT):

            @pl.when(position >= here)
            def _():
                traces[line, position] = jnp.zeros((6, FACE, R), BF16)

    squares[...] = jnp.zeros_like(squares)

    def body(slot, line, position):
        values = vector[line, position]
        product[line, position] = jnp.dot(diagonal[line, position], values, preferred_element_type=F32)
        whole = values.astype(F32)
        squares[...] += partial(whole * whole)
        for half in range(2):
            columns = slice(half * HALF, (half + 1) * HALF)
            wide[half] = whole[:, columns]
            for face, first in ((0, 0), (1, 3)):
                traces[line, position, face, :, columns] = wide[half, pl.ds(first, FACE, stride=4), :].astype(BF16)
        traces[line, position, 2] = a_face(values, 0)
        traces[line, position, 3] = a_face(values, 3)
        runs = whole.reshape(10, 4, 8, R)
        upper = lax.broadcasted_iota(jnp.int32, (10, 8, R), 1) < 4
        south = jnp.where(upper, runs[:, 0], pltpu.roll(runs[:, 2], 4, axis=1))
        north = jnp.where(upper, pltpu.roll(runs[:, 1], 4, axis=1), runs[:, 3])
        traces[line, position, 4] = south.reshape(FACE, R).astype(BF16)
        traces[line, position, 5] = north.reshape(FACE, R).astype(BF16)

    for_listed(lengths, listed, list_living(lengths, listed), body)
    for copy in copies:
        copy.wait()


def product_kernel(
    tile,
    traces,
    over_core,
    over_y,
    over_pair,
    over_next,
    lower,
    lifting,
    inverse,
    steps,
    map_here,
    map_y,
    product_in,
    product,
    carries,
    outgoing,
    listed,
    driven,
):
    core, odd = lax.axis_index("core"), lax.axis_index("z") % 2
    lengths, norths = lengths_and_norths(tile)
    zero = jnp.zeros((FACE, R), BF16)

    def multiply(slot, line, position):
        wall_slot = jnp.minimum(slot, MOVING - 1)
        moving = slot < MOVING
        from_core = jnp.where(moving, over_core[wall_slot], zero)
        from_y = jnp.where(moving, over_y[wall_slot], zero)
        below_edge = jnp.where(core == 0, from_y, from_core)
        above_edge = jnp.where(core == 0, from_core, from_y)
        below = jnp.where(position == 0, below_edge, traces[line, jnp.maximum(position - 1, 0), 1])
        above = jnp.where(
            position == SEGMENT - 1, above_edge, traces[line, jnp.minimum(position + 1, SEGMENT - 1), 0]
        )
        west_edge = jnp.where(odd == 0, over_next[position], over_pair[position])
        east_edge = jnp.where(odd == 0, over_pair[position], over_next[position])
        west = jnp.where(line == 0, west_edge, traces[jnp.maximum(line - 1, 0), position, 3])
        east = jnp.where(
            line == LINES_HERE - 1, east_edge, traces[jnp.minimum(line + 1, LINES_HERE - 1), position, 2]
        )
        north_line = norths[line]
        south_line = jnp.int32(0)
        for other in range(1, LINES_HERE):
            south_line = jnp.where(norths[other] == line, other, south_line)
        south = traces[south_line, position, 5]
        north = traces[north_line, position, 4]
        neighbours = jnp.concatenate([below, above, west, east, south, north], axis=0)
        upper_blocks = lifting[line, position].reshape(5 * FACE, BLOCK)
        blocks = jnp.concatenate([lower[line, position], upper_blocks], axis=0)
        product[line, position] = product_in[line, position] + transposed_times(blocks, neighbours)

    count = list_living(lengths, listed)
    for_listed(lengths, listed, count, multiply)

    for slot in range(MOVING):
        for position in range(SEGMENT):

            @pl.when(position >= living_here(lengths, line_in_slot(slot, shortest_line(lengths))))
            def _():
                driven[slot, position] = jnp.zeros((FACE, R), F32)

    def drive(slot, line, position):
        high, low = split_exactly(product[line, position])
        rows = inverse[line, position]
        tail = rows[:, 256:]
        driven[slot, position] = jnp.dot(
            jnp.concatenate([rows[:, :256], rows[:, :256], tail, tail], axis=1),
            jnp.concatenate([high[:256], low[:256], high[256:], low[256:]], axis=0),
            preferred_element_type=F32,
        )

    for_listed(lengths, listed, list_living(lengths, listed, MOVING), drive)
    carried = [driven[slot, 0] for slot in range(MOVING)]
    for position in range(1, SEGMENT):
        for slot in range(MOVING):
            carries[slot, position - 1] = carried[slot]
            carried[slot] = driven[slot, position] + mapped(steps[slot, position], carried[slot])
    for slot in range(MOVING):
        outgoing[slot] = carried[slot]
    outgoing[OWN_MAPS] = map_here[...]
    outgoing[Y_MAPS] = map_y[...]


def map_of(maps, slot):
    return maps[:, slot * FACE : (slot + 1) * FACE]


def chip_kernel(mine, other, near, far):
    core, y = lax.axis_index("core"), lax.axis_index("y")
    second_maps = jnp.where(core == 0, other[OWN_MAPS], mine[OWN_MAPS])
    values = []
    for slot in range(MOVING):
        own, away = mine[slot], other[slot]
        first_value = jnp.where(core == 0, own[:, :HALF], away[:, HALF:])
        second_value = jnp.where(core == 0, away[:, :HALF], own[:, HALF:])
        values.append(mapped(map_of(second_maps, slot), first_value) + second_value)
    for slot in range(MOVING):
        near[slot] = values[slot]
        far[slot] = values[slot]

    @pl.when(y == 0)
    def _():
        through_chip(mine, other, values, far)


def through_chip(mine, other, values, results):
    core = lax.axis_index("core")
    first_maps = jnp.where(core == 0, mine[Y_MAPS], other[Y_MAPS])
    second_maps = jnp.where(core == 0, other[Y_MAPS], mine[Y_MAPS])
    moved = [mapped(map_of(first_maps, slot), value) for slot, value in enumerate(values)]
    for slot, value in enumerate(moved):
        results[slot] = mapped(map_of(second_maps, slot), value)


def arriving_kernel(one, two, three, mine, other, arriving):
    y = lax.axis_index("y")
    below = [two[slot] + three[slot] for slot in range(MOVING)]
    for slot in range(MOVING):
        arriving[slot] = below[slot]

    @pl.when(y == 3)
    def _():
        through_chip(mine, other, below, arriving)

    for slot in range(MOVING):
        arriving[slot] = arriving[slot] + one[slot]


def eliminate_kernel(
    tile,
    vector,
    squares,
    product,
    lower,
    prefixes,
    carries,
    mine,
    other,
    beside,
    eliminated,
    tiles,
    listed,
    entering,
    sums,
):
    core = lax.axis_index("core")
    lengths, _ = lengths_and_norths(tile)
    entering[...] = jnp.zeros_like(entering)
    values = []
    for slot in range(MOVING):
        left = jnp.where(core == 0, mine[slot], other[slot])
        right = jnp.where(core == 0, other[slot], mine[slot])
        value = jnp.concatenate([left, right], axis=1)
        passed = mapped(map_of(beside[OWN_MAPS], slot), value) + beside[slot]
        values.append(jnp.where(core == 0, value, passed))
    for slot, value in enumerate(values):
        entering[slot, 0] = value
        moved = mapped(prefixes[slot].reshape((SEGMENT - 1) * FACE, FACE), value)
        for position in range(1, SEGMENT):
            entering[slot, position] = carries[slot, position - 1] + moved[(position - 1) * FACE : position * FACE]

    count = list_living(lengths, listed)
    sums[...] = jnp.zeros_like(sums)

    def correct(slot, line, position):
        high, low = split_exactly(entering[slot, position])
        block = lower[line, position]
        correction = transposed_times(jnp.concatenate([block, block], axis=0), jnp.concatenate([high, low], axis=0))
        value = product[line, position] - correction
        eliminated[line, position] = value
        masked = vector[line, position].astype(F32)
        sums[0] += partial(masked * value)

    for_listed(lengths, listed, count, correct)
    cross = sums[0].sum(axis=0, keepdims=True)
    square = squares[...].sum(axis=0, keepdims=True)
    share = jnp.where(square > 0, cross / square, 0.0)

    def leave(slot, line, position):
        rest = eliminated[line, position] - share * vector[line, position].astype(F32)
        sums[1] += partial(rest * rest)

    for_listed(lengths, listed, count, leave)
    rest = sums[1].sum(axis=0, keepdims=True)
    pieces = [part[:, at : at + HALF] for part in (cross, square, rest) for at in (0, HALF)]
    sums_tile = jnp.concatenate(pieces + [jnp.zeros((2, HALF), F32)], axis=0)
    for copy in range(tiles.shape[0]):
        tiles[copy] = sums_tile


def merged(tiles):
    cross, square, rest = tiles[:, 0:2], tiles[:, 2:4], tiles[:, 4:6]
    all_cross, all_square = cross.sum(axis=0), square.sum(axis=0)
    own = jnp.where(square > 0, cross / square, 0.0)
    ratio = all_cross / all_square
    away = jnp.where(square > 0, own - ratio[None], 0.0)
    all_rest = (rest + (square * away) * away).sum(axis=0)
    return all_cross, all_square, all_rest, ratio


def merge_kernel(tiles_in, tiles):
    cross, square, rest, _ = merged(tiles_in[...])
    tile = jnp.concatenate([cross, square, rest, jnp.zeros((2, HALF), F32)], axis=0)
    for copy in range(tiles.shape[0]):
        tiles[copy] = tile


def finish_kernel(entries, tile, tiles, vector, eliminated, basis, coefs, held, sems):
    lengths, _ = lengths_and_norths(tile)
    _, _, rest, ratio = merged(tiles[...])
    spread = jnp.sqrt(rest / entries + 1e-06)
    ratio = jnp.concatenate([ratio[0:1], ratio[1:2]], axis=1)
    spread = jnp.concatenate([spread[0:1], spread[1:2]], axis=1)
    coefs[...] = jnp.concatenate([ratio, spread], axis=0)
    scale = 1.0 / spread
    copies = []
    for line in range(LINES_HERE):
        here = living_here(lengths, line)
        for position in range(SEGMENT):
            masked = vector[line, position].astype(F32)
            value = (eliminated[line, position] - ratio * masked) * scale
            held[line, position] = jnp.where(position < here, value, 0.0).astype(BF16)
        copy = pltpu.make_async_copy(held.at[line], basis.at[line], sems.at[line])
        copy.start()
        copies.append(copy)
    for copy in copies:
        copy.wait()


def call(kernel, outs, ins, scratch=(), limit=12, flops=0, moved=0, out_specs=None, in_hbm=()):
    return pl.pallas_call(
        kernel,
        out_shape=outs,
        in_specs=[
            pl.BlockSpec(memory_space=pltpu.HBM) if at in in_hbm else in_vmem()
            for at, arg in enumerate(ins)
        ],
        out_specs=out_specs or jax.tree.map(lambda _: in_vmem(), outs),
        scratch_shapes=list(scratch),
        compiler_params=pltpu.CompilerParams(vmem_limit_bytes=limit * 2**20),
        cost_estimate=pl.CostEstimate(flops=flops, bytes_accessed=moved, transcendentals=0),
        name=getattr(kernel, "__name__", "finish_kernel"),
    )(*[pltpu.with_memory_space_constraint(arg, pltpu.HBM) if at in in_hbm else arg for at, arg in enumerate(ins)])


def shaped(*shape, dtype=F32):
    return jax.ShapeDtypeStruct(shape, dtype)


LISTED = pltpu.SMEM((LINES_HERE * SEGMENT + 1,), jnp.int32)


def per_device(vector, lengths, north_of, diagonal, lifting, inverse_rows):
    edge = shaped(MOVING, FACE, R, dtype=BF16)
    side = shaped(SEGMENT, FACE, R, dtype=BF16)
    blocks = shaped(LINES_HERE, SEGMENT, FACE, BLOCK, dtype=BF16)
    over_core, over_y, over_pair, over_next, steps, prefixes, whole, lower, inverse, vector, tile = call(
        edges_kernel,
        (
            edge,
            edge,
            side,
            side,
            shaped(MOVING, SEGMENT, FACE, FACE),
            shaped(MOVING, SEGMENT - 1, FACE, FACE),
            shaped(FACE, R),
            blocks,
            blocks,
            shaped(LINES_HERE, SEGMENT, BLOCK, R, dtype=BF16),
            shaped(16, HALF),
        ),
        (lengths, north_of, vector, lifting, inverse_rows),
        (
            pltpu.SMEM((LINES_HERE,), jnp.int32),
            pltpu.SMEM((1, LINES_HERE), jnp.int32),
            pltpu.SemaphoreType.DMA((2,)),
            pltpu.SemaphoreType.DMA((3, LINES_HERE)),
        ),
        in_hbm=(0, 1, 2, 3, 4),
    )
    walls, surfs = lax.axis_size(WALL), lax.axis_size(SURF)
    swap = [(0, 1), (1, 0)]
    over_core = lax.ppermute(over_core, "core", swap)
    rungs = [(i, i + 1) for i in range(1, walls - 1, 2)]
    over_y = lax.ppermute(over_y, WALL, rungs + [(b, a) for a, b in rungs])
    over_pair = lax.ppermute(over_pair, SURF, [(i, i ^ 1) for i in range(surfs)])
    nexts = [(i, (i + 1) % surfs) for i in range(1, surfs, 2)]
    over_next = lax.ppermute(over_next, SURF, nexts + [(b, a) for a, b in nexts])

    map_y = lax.ppermute(whole, "y", [(1, 0), (2, 3)])
    product, traces, lifting_here, squares = call(
        diagonal_kernel,
        (
            shaped(LINES_HERE, SEGMENT, BLOCK, R),
            shaped(LINES_HERE, SEGMENT, 6, FACE, R, dtype=BF16),
            shaped(LINES_HERE, SEGMENT, 5, FACE, BLOCK, dtype=BF16),
            shaped(8, R),
        ),
        (tile, vector, diagonal, lifting),
        (LISTED, pltpu.VMEM((2, BLOCK, HALF), F32), pltpu.SemaphoreType.DMA((LINES_HERE,))),
        in_hbm=(3,),
    )
    product, carries, outgoing = call(
        product_kernel,
        (
            shaped(LINES_HERE, SEGMENT, BLOCK, R),
            shaped(MOVING, SEGMENT - 1, FACE, R),
            shaped(MOVING + 2, FACE, R),
        ),
        (
            tile,
            traces,
            over_core,
            over_y,
            over_pair,
            over_next,
            lower,
            lifting_here,
            inverse,
            steps,
            whole,
            map_y,
            product,
        ),
        (LISTED, pltpu.VMEM((LINES_HERE, SEGMENT, FACE, R), F32)),
    )
    ranks = lax.axis_size("y")

    def up_chips(value, far):
        return lax.ppermute(value, "y", [(i, i + far) for i in range(ranks - far)])

    beside = lax.ppermute(outgoing, "core", swap)
    near, far = call(chip_kernel, (shaped(MOVING, FACE, HALF), shaped(MOVING, FACE, HALF)), (outgoing, beside))
    one, two, three = up_chips(near, 1), up_chips(far, 2), up_chips(far, 3)
    arriving = call(arriving_kernel, shaped(MOVING, FACE, HALF), (one, two, three, outgoing, beside))
    arriving_beside = lax.ppermute(arriving, "core", swap)
    eliminated, tiles = call(
        eliminate_kernel,
        (shaped(LINES_HERE, SEGMENT, BLOCK, R), shaped(surfs, 8, HALF)),
        (tile, vector, squares, product, lower, prefixes, carries, arriving, arriving_beside, beside),
        (LISTED, pltpu.VMEM((LINES_HERE, SEGMENT, FACE, R), F32), pltpu.VMEM((2, 8, R), F32)),
        flops=10**9,
        moved=10**7,
    )
    tiles = lax.all_to_all(tiles, SURF, 0, 0, tiled=True)
    tiles = call(merge_kernel, shaped(walls, 8, HALF), (tiles,))
    tiles = lax.all_to_all(tiles, WALL, 0, 0, tiled=True)
    entries = LINES_HERE * SEGMENT * BLOCK * walls * surfs
    return call(
        functools.partial(finish_kernel, entries),
        (shaped(LINES_HERE, SEGMENT, BLOCK, R, dtype=BF16), shaped(2, R)),
        (tile, tiles, vector, eliminated),
        (pltpu.VMEM((LINES_HERE, SEGMENT, BLOCK, R), BF16), pltpu.SemaphoreType.DMA((LINES_HERE,))),
        out_specs=(pl.BlockSpec(memory_space=pl.ANY), in_vmem()),
    )


def solution(mesh):
    split = Mesh(mesh.devices.reshape(4, 2, 4, 8), ("y", "core", "x", "z"))
    placed = (
        P(SURF, WALL, None, None),
        P(SURF),
        P(SURF, None),
        P(SURF, WALL, None, None),
        P(SURF, WALL, None, None, None),
        P(SURF, WALL, None, None),
    )
    return jax.shard_map(
        per_device,
        mesh=split,
        in_specs=placed,
        out_specs=(P(SURF, WALL, None, None), P()),
        check_vma=False,
    )
```

```python
import functools

import jax
import jax.numpy as jnp
from jax import lax
from jax.experimental import pallas as pl
from jax.experimental.pallas import tpu as pltpu
from jax.sharding import Mesh
from jax.sharding import PartitionSpec as P

BLOCK = 320
FACE = 80
LINES_HERE = 4
SEGMENT = 4
MOVING = 3
R = 256
HALF = 128
OWN_MAPS, Y_MAPS = MOVING, MOVING + 1
WALL = ("y", "core")
SURF = ("x", "z")
F32 = jnp.float32
BF16 = jnp.bfloat16
EXACT = lax.Precision.HIGHEST
VMEM = pltpu.VMEM


def in_vmem():
    return pl.BlockSpec(memory_space=VMEM)


class Digits:
    def __init__(self, number, bits):
        self.number, self.bits = number, bits

    def __getitem__(self, at):
        return (self.number >> (self.bits * at)) & ((1 << self.bits) - 1)


def lengths_and_norths(tile):
    return Digits(jnp.max(tile[0:8]).astype(jnp.int32), 6), Digits(jnp.max(tile[8:16]).astype(jnp.int32), 2)


def wall_here():
    return lax.axis_index("y") * 2 + lax.axis_index("core")


def living_here(lengths, line):
    return jnp.clip(lengths[line] - SEGMENT * wall_here(), 0, SEGMENT)


def shortest_line(lengths):
    at = jnp.int32(3)
    for line in (2, 1, 0):
        at = jnp.where(lengths[line] == 1, line, at)
    return at


def line_in_slot(slot, short):
    return jnp.where(slot == MOVING, short, slot + (slot >= short).astype(jnp.int32))


def list_living(lengths, listed, slots=LINES_HERE):
    short = shortest_line(lengths)
    count = jnp.int32(0)
    for slot in range(slots):
        here = living_here(lengths, line_in_slot(slot, short))
        for position in range(SEGMENT):
            listed[count] = slot * SEGMENT + position
            count = count + (position < here).astype(jnp.int32)
    return count


def for_listed(lengths, listed, count, body, together=4):
    short = shortest_line(lengths)

    def one(trip):
        entry = listed[trip]
        slot = entry // SEGMENT
        body(slot, line_in_slot(slot, short), entry % SEGMENT)

    def group(first, size):
        for part in range(size):
            one(first + part)

    whole = count // together

    @pl.loop(0, whole)
    def _(trip):
        group(trip * together, together)

    @pl.loop(whole * together, count)
    def _(trip):
        group(trip, 1)


def wall_face_rows():
    row = lax.broadcasted_iota(jnp.int32, (2 * FACE, BLOCK), 0)
    column = lax.broadcasted_iota(jnp.int32, (2 * FACE, BLOCK), 1)
    second = (row >= FACE).astype(jnp.int32)
    return (column == 4 * (row - FACE * second) + 3 * second).astype(BF16)


def pick(rows, values):
    return jnp.dot(rows, values, preferred_element_type=F32).astype(BF16)


def a_face(block, end):
    return jnp.concatenate([block[64 * v + 16 * end : 64 * v + 16 * end + 16] for v in range(5)], axis=0)


def partial(values):
    return values.reshape(BLOCK // 8, 8, R).sum(axis=0)


def split_exactly(values):
    high = values.astype(BF16)
    low = (values - high.astype(F32)).astype(BF16)
    return high, low


def transposed_times(left, right):
    return lax.dot_general(left, right, (((0,), (0,)), ((), ())), preferred_element_type=F32)


def mapped(matrix, state):
    matrix_high, matrix_low = split_exactly(matrix)
    high, low = split_exactly(state)
    rows = matrix.shape[0]
    both = jnp.dot(jnp.concatenate([matrix_high, matrix_low], axis=0), high, preferred_element_type=F32)
    return both[:rows] + (both[rows:] + jnp.dot(matrix_high, low, preferred_element_type=F32))


def edges_kernel(
    lengths_hbm,
    norths_hbm,
    vector_hbm,
    lifting_hbm,
    inverse_hbm,
    over_core,
    over_y,
    over_pair,
    over_next,
    steps,
    prefixes,
    whole,
    lower,
    inverse,
    vector,
    tile,
    alive,
    lengths,
    norths,
    sems,
    block_sems,
):
    core, odd = lax.axis_index("core"), lax.axis_index("z") % 2
    copies = [
        pltpu.make_async_copy(lengths_hbm, lengths, sems.at[0]),
        pltpu.make_async_copy(norths_hbm, norths, sems.at[1]),
    ]
    for line in range(LINES_HERE):
        copies.append(pltpu.make_async_copy(vector_hbm.at[line], vector.at[line], block_sems.at[2, line]))
    needed = []
    for line in range(LINES_HERE):
        needed.append(pltpu.make_async_copy(inverse_hbm.at[line], inverse.at[line], block_sems.at[0, line]))
        needed.append(pltpu.make_async_copy(lifting_hbm.at[line, :, 0], lower.at[line], block_sems.at[1, line]))
    for copy in copies + needed:
        copy.start()
    rows = wall_face_rows()
    for copy in copies:
        copy.wait()
    length_digits, north_digits = jnp.int32(0), jnp.int32(0)
    for line in range(LINES_HERE):
        length_digits = length_digits + (lengths[line] << (6 * line))
        north_digits = north_digits + (norths[0, line] << (2 * line))
    tile[0:8] = jnp.full((8, HALF), length_digits.astype(F32))
    tile[8:16] = jnp.full((8, HALF), north_digits.astype(F32))
    for line in range(LINES_HERE):
        here = living_here(lengths, line)
        for position in range(SEGMENT):
            alive[line, position] = jnp.full((8, HALF), (position < here).astype(jnp.int32).astype(F32))
    short = shortest_line(lengths)
    zero = jnp.zeros((FACE, R), BF16)
    for slot in range(MOVING):
        line = line_in_slot(slot, short)
        here = living_here(lengths, line)
        down = jnp.where(here > 0, pick(rows[:FACE], vector[line, 0]), zero)
        up = jnp.where(here > SEGMENT - 1, pick(rows[FACE:], vector[line, SEGMENT - 1]), zero)
        over_core[slot] = jnp.where(core == 0, up, down)
        over_y[slot] = jnp.where(core == 0, down, up)
    first, last = living_here(lengths, 0), living_here(lengths, LINES_HERE - 1)
    for position in range(SEGMENT):
        from_first = jnp.where(position < first, a_face(vector[0, position], 0), zero)
        from_last = jnp.where(position < last, a_face(vector[LINES_HERE - 1, position], 3), zero)
        over_pair[position] = jnp.where(odd == 0, from_last, from_first)
        over_next[position] = jnp.where(odd == 0, from_first, from_last)
    for copy in needed:
        copy.wait()
    lines = [line_in_slot(slot, short) for slot in range(MOVING)]
    so_far = [None] * MOVING
    for position in range(SEGMENT):
        for slot, line in enumerate(lines):
            step = lax.dot_general(
                inverse[line, position],
                lower[line, position],
                (((1,), (1,)), ((), ())),
                preferred_element_type=F32,
            )
            steps[slot, position] = jnp.where(position < living_here(lengths, line), -step, 0.0)
    for position in range(SEGMENT):
        for slot in range(MOVING):
            step = steps[slot, position]
            so_far[slot] = step if position == 0 else mapped(step, so_far[slot])
            if position < SEGMENT - 1:
                prefixes[slot, position] = so_far[slot]
    whole[...] = jnp.concatenate(so_far + [jnp.zeros((FACE, R - MOVING * FACE), F32)], axis=1)


def diagonal_kernel(tile, vector, diagonal, product, traces, squares, listed, wide):
    lengths, _ = lengths_and_norths(tile)
    for line in range(LINES_HERE):
        here = living_here(lengths, line)
        for position in range(SEGMENT):

            @pl.when(position >= here)
            def _():
                traces[line, position] = jnp.zeros((6, FACE, R), BF16)

    squares[...] = jnp.zeros_like(squares)

    def body(slot, line, position):
        values = vector[line, position]
        product[line, position] = jnp.dot(diagonal[line, position], values, preferred_element_type=F32)
        whole = values.astype(F32)
        squares[...] += partial(whole * whole)
        for half in range(2):
            columns = slice(half * HALF, (half + 1) * HALF)
            wide[half] = whole[:, columns]
            for face, first in ((0, 0), (1, 3)):
                traces[line, position, face, :, columns] = wide[half, pl.ds(first, FACE, stride=4), :].astype(BF16)
        traces[line, position, 2] = a_face(values, 0)
        traces[line, position, 3] = a_face(values, 3)
        runs = whole.reshape(10, 4, 8, R)
        upper = lax.broadcasted_iota(jnp.int32, (10, 8, R), 1) < 4
        south = jnp.where(upper, runs[:, 0], pltpu.roll(runs[:, 2], 4, axis=1))
        north = jnp.where(upper, pltpu.roll(runs[:, 1], 4, axis=1), runs[:, 3])
        traces[line, position, 4] = south.reshape(FACE, R).astype(BF16)
        traces[line, position, 5] = north.reshape(FACE, R).astype(BF16)

    for_listed(lengths, listed, list_living(lengths, listed), body)


def product_kernel(
    tile,
    traces,
    over_core,
    over_y,
    over_pair,
    over_next,
    lifting,
    inverse,
    steps,
    map_here,
    map_y,
    product_in,
    product,
    carries,
    outgoing,
    listed,
    driven,
):
    core, odd = lax.axis_index("core"), lax.axis_index("z") % 2
    lengths, norths = lengths_and_norths(tile)
    zero = jnp.zeros((FACE, R), BF16)

    def multiply(slot, line, position):
        wall_slot = jnp.minimum(slot, MOVING - 1)
        moving = slot < MOVING
        from_core = jnp.where(moving, over_core[wall_slot], zero)
        from_y = jnp.where(moving, over_y[wall_slot], zero)
        below_edge = jnp.where(core == 0, from_y, from_core)
        above_edge = jnp.where(core == 0, from_core, from_y)
        below = jnp.where(position == 0, below_edge, traces[line, jnp.maximum(position - 1, 0), 1])
        above = jnp.where(
            position == SEGMENT - 1, above_edge, traces[line, jnp.minimum(position + 1, SEGMENT - 1), 0]
        )
        west_edge = jnp.where(odd == 0, over_next[position], over_pair[position])
        east_edge = jnp.where(odd == 0, over_pair[position], over_next[position])
        west = jnp.where(line == 0, west_edge, traces[jnp.maximum(line - 1, 0), position, 3])
        east = jnp.where(
            line == LINES_HERE - 1, east_edge, traces[jnp.minimum(line + 1, LINES_HERE - 1), position, 2]
        )
        north_line = norths[line]
        south_line = jnp.int32(0)
        for other in range(1, LINES_HERE):
            south_line = jnp.where(norths[other] == line, other, south_line)
        south = traces[south_line, position, 5]
        north = traces[north_line, position, 4]
        neighbours = jnp.concatenate([below, above, west, east, south, north], axis=0)
        blocks = lifting[line, position].reshape(6 * FACE, BLOCK)
        product[line, position] = product_in[line, position] + transposed_times(blocks, neighbours)

    count = list_living(lengths, listed)
    for_listed(lengths, listed, count, multiply)

    for slot in range(MOVING):
        for position in range(SEGMENT):

            @pl.when(position >= living_here(lengths, line_in_slot(slot, shortest_line(lengths))))
            def _():
                driven[slot, position] = jnp.zeros((FACE, R), F32)

    def drive(slot, line, position):
        high, low = split_exactly(product[line, position])
        rows = inverse[line, position]
        tail = rows[:, 256:]
        driven[slot, position] = jnp.dot(
            jnp.concatenate([rows[:, :256], rows[:, :256], tail, tail], axis=1),
            jnp.concatenate([high[:256], low[:256], high[256:], low[256:]], axis=0),
            preferred_element_type=F32,
        )

    for_listed(lengths, listed, list_living(lengths, listed, MOVING), drive)
    carried = [driven[slot, 0] for slot in range(MOVING)]
    for position in range(1, SEGMENT):
        for slot in range(MOVING):
            carries[slot, position - 1] = carried[slot]
            carried[slot] = driven[slot, position] + mapped(steps[slot, position], carried[slot])
    for slot in range(MOVING):
        outgoing[slot] = carried[slot]
    outgoing[OWN_MAPS] = map_here[...]
    outgoing[Y_MAPS] = map_y[...]


def map_of(maps, slot):
    return maps[:, slot * FACE : (slot + 1) * FACE]


def chip_kernel(mine, other, near, far):
    core, y = lax.axis_index("core"), lax.axis_index("y")
    second_maps = jnp.where(core == 0, other[OWN_MAPS], mine[OWN_MAPS])
    values = []
    for slot in range(MOVING):
        own, away = mine[slot], other[slot]
        first_value = jnp.where(core == 0, own[:, :HALF], away[:, HALF:])
        second_value = jnp.where(core == 0, away[:, :HALF], own[:, HALF:])
        values.append(mapped(map_of(second_maps, slot), first_value) + second_value)
    for slot in range(MOVING):
        near[slot] = values[slot]
        far[slot] = values[slot]

    @pl.when(y == 0)
    def _():
        through_chip(mine, other, values, far)


def through_chip(mine, other, values, results):
    core = lax.axis_index("core")
    first_maps = jnp.where(core == 0, mine[Y_MAPS], other[Y_MAPS])
    second_maps = jnp.where(core == 0, other[Y_MAPS], mine[Y_MAPS])
    moved = [mapped(map_of(first_maps, slot), value) for slot, value in enumerate(values)]
    for slot, value in enumerate(moved):
        results[slot] = mapped(map_of(second_maps, slot), value)


def arriving_kernel(one, two, three, mine, other, arriving):
    y = lax.axis_index("y")
    below = [two[slot] + three[slot] for slot in range(MOVING)]
    for slot in range(MOVING):
        arriving[slot] = below[slot]

    @pl.when(y == 3)
    def _():
        through_chip(mine, other, below, arriving)

    for slot in range(MOVING):
        arriving[slot] = arriving[slot] + one[slot]


def eliminate_kernel(
    tile,
    vector,
    squares,
    product,
    lower,
    prefixes,
    carries,
    mine,
    other,
    beside,
    eliminated,
    tiles,
    listed,
    entering,
    sums,
):
    core = lax.axis_index("core")
    lengths, _ = lengths_and_norths(tile)
    entering[...] = jnp.zeros_like(entering)
    values = []
    for slot in range(MOVING):
        left = jnp.where(core == 0, mine[slot], other[slot])
        right = jnp.where(core == 0, other[slot], mine[slot])
        value = jnp.concatenate([left, right], axis=1)
        passed = mapped(map_of(beside[OWN_MAPS], slot), value) + beside[slot]
        values.append(jnp.where(core == 0, value, passed))
    for slot, value in enumerate(values):
        entering[slot, 0] = value
        moved = mapped(prefixes[slot].reshape((SEGMENT - 1) * FACE, FACE), value)
        for position in range(1, SEGMENT):
            entering[slot, position] = carries[slot, position - 1] + moved[(position - 1) * FACE : position * FACE]

    count = list_living(lengths, listed)
    sums[...] = jnp.zeros_like(sums)

    def correct(slot, line, position):
        high, low = split_exactly(entering[slot, position])
        block = lower[line, position]
        correction = transposed_times(jnp.concatenate([block, block], axis=0), jnp.concatenate([high, low], axis=0))
        value = product[line, position] - correction
        eliminated[line, position] = value
        masked = vector[line, position].astype(F32)
        sums[0] += partial(masked * value)

    for_listed(lengths, listed, count, correct)
    cross = sums[0].sum(axis=0, keepdims=True)
    square = squares[...].sum(axis=0, keepdims=True)
    share = jnp.where(square > 0, cross / square, 0.0)

    def leave(slot, line, position):
        rest = eliminated[line, position] - share * vector[line, position].astype(F32)
        sums[1] += partial(rest * rest)

    for_listed(lengths, listed, count, leave)
    rest = sums[1].sum(axis=0, keepdims=True)
    pieces = [part[:, at : at + HALF] for part in (cross, square, rest) for at in (0, HALF)]
    sums_tile = jnp.concatenate(pieces + [jnp.zeros((2, HALF), F32)], axis=0)
    for copy in range(tiles.shape[0]):
        tiles[copy] = sums_tile


def merged(tiles):
    cross, square, rest = tiles[:, 0:2], tiles[:, 2:4], tiles[:, 4:6]
    all_cross, all_square = cross.sum(axis=0), square.sum(axis=0)
    own = jnp.where(square > 0, cross / square, 0.0)
    ratio = all_cross / all_square
    away = jnp.where(square > 0, own - ratio[None], 0.0)
    all_rest = (rest + (square * away) * away).sum(axis=0)
    return all_cross, all_square, all_rest, ratio


def merge_kernel(tiles_in, tiles):
    cross, square, rest, _ = merged(tiles_in[...])
    tile = jnp.concatenate([cross, square, rest, jnp.zeros((2, HALF), F32)], axis=0)
    for copy in range(tiles.shape[0]):
        tiles[copy] = tile


def finish_kernel(entries, alive, tiles, vector, eliminated, basis, coefs, held, sems):
    _, _, rest, ratio = merged(tiles[...])
    spread = jnp.sqrt(rest / entries + 1e-06)
    ratio = jnp.concatenate([ratio[0:1], ratio[1:2]], axis=1)
    spread = jnp.concatenate([spread[0:1], spread[1:2]], axis=1)
    coefs[...] = jnp.concatenate([ratio, spread], axis=0)
    scale = 1.0 / spread
    copies = []
    for line in range(LINES_HERE):
        for position in range(SEGMENT):
            masked = vector[line, position].astype(F32)
            value = (eliminated[line, position] - ratio * masked) * scale
            flags = alive[line, position]
            flags = jnp.concatenate([flags, flags], axis=1) > 0
            value = jnp.where(flags[None], value.reshape(BLOCK // 8, 8, R), 0.0)
            held[line, position] = value.reshape(BLOCK, R).astype(BF16)
        copy = pltpu.make_async_copy(held.at[line], basis.at[line], sems.at[line])
        copy.start()
        copies.append(copy)
    for copy in copies:
        copy.wait()


def call(kernel, outs, ins, scratch=(), limit=12, flops=0, moved=0, out_specs=None, in_hbm=()):
    return pl.pallas_call(
        kernel,
        out_shape=outs,
        in_specs=[
            pl.BlockSpec(memory_space=pltpu.HBM) if at in in_hbm else in_vmem()
            for at, arg in enumerate(ins)
        ],
        out_specs=out_specs or jax.tree.map(lambda _: in_vmem(), outs),
        scratch_shapes=list(scratch),
        compiler_params=pltpu.CompilerParams(vmem_limit_bytes=limit * 2**20),
        cost_estimate=pl.CostEstimate(flops=flops, bytes_accessed=moved, transcendentals=0),
        name=getattr(kernel, "__name__", "finish_kernel"),
    )(*[pltpu.with_memory_space_constraint(arg, pltpu.HBM) if at in in_hbm else arg for at, arg in enumerate(ins)])


def shaped(*shape, dtype=F32):
    return jax.ShapeDtypeStruct(shape, dtype)


LISTED = pltpu.SMEM((LINES_HERE * SEGMENT + 1,), jnp.int32)


def per_device(vector, lengths, north_of, diagonal, lifting, inverse_rows):
    edge = shaped(MOVING, FACE, R, dtype=BF16)
    side = shaped(SEGMENT, FACE, R, dtype=BF16)
    blocks = shaped(LINES_HERE, SEGMENT, FACE, BLOCK, dtype=BF16)
    over_core, over_y, over_pair, over_next, steps, prefixes, whole, lower, inverse, vector, tile, alive = call(
        edges_kernel,
        (
            edge,
            edge,
            side,
            side,
            shaped(MOVING, SEGMENT, FACE, FACE),
            shaped(MOVING, SEGMENT - 1, FACE, FACE),
            shaped(FACE, R),
            blocks,
            blocks,
            shaped(LINES_HERE, SEGMENT, BLOCK, R, dtype=BF16),
            shaped(16, HALF),
            shaped(LINES_HERE, SEGMENT, 8, HALF),
        ),
        (lengths, north_of, vector, lifting, inverse_rows),
        (
            pltpu.SMEM((LINES_HERE,), jnp.int32),
            pltpu.SMEM((1, LINES_HERE), jnp.int32),
            pltpu.SemaphoreType.DMA((2,)),
            pltpu.SemaphoreType.DMA((3, LINES_HERE)),
        ),
        in_hbm=(0, 1, 2, 3, 4),
    )
    walls, surfs = lax.axis_size(WALL), lax.axis_size(SURF)
    swap = [(0, 1), (1, 0)]
    over_core = lax.ppermute(over_core, "core", swap)
    rungs = [(i, i + 1) for i in range(1, walls - 1, 2)]
    over_y = lax.ppermute(over_y, WALL, rungs + [(b, a) for a, b in rungs])
    over_pair = lax.ppermute(over_pair, SURF, [(i, i ^ 1) for i in range(surfs)])
    nexts = [(i, (i + 1) % surfs) for i in range(1, surfs, 2)]
    over_next = lax.ppermute(over_next, SURF, nexts + [(b, a) for a, b in nexts])

    map_y = lax.ppermute(whole, "y", [(1, 0), (2, 3)])
    product, traces, squares = call(
        diagonal_kernel,
        (
            shaped(LINES_HERE, SEGMENT, BLOCK, R),
            shaped(LINES_HERE, SEGMENT, 6, FACE, R, dtype=BF16),
            shaped(8, R),
        ),
        (tile, vector, diagonal),
        (LISTED, pltpu.VMEM((2, BLOCK, HALF), F32)),
    )
    product, carries, outgoing = call(
        product_kernel,
        (
            shaped(LINES_HERE, SEGMENT, BLOCK, R),
            shaped(MOVING, SEGMENT - 1, FACE, R),
            shaped(MOVING + 2, FACE, R),
        ),
        (
            tile,
            traces,
            over_core,
            over_y,
            over_pair,
            over_next,
            lifting,
            inverse,
            steps,
            whole,
            map_y,
            product,
        ),
        (LISTED, pltpu.VMEM((LINES_HERE, SEGMENT, FACE, R), F32)),
    )
    ranks = lax.axis_size("y")

    def up_chips(value, far):
        return lax.ppermute(value, "y", [(i, i + far) for i in range(ranks - far)])

    beside = lax.ppermute(outgoing, "core", swap)
    near, far = call(chip_kernel, (shaped(MOVING, FACE, HALF), shaped(MOVING, FACE, HALF)), (outgoing, beside))
    one, two, three = up_chips(near, 1), up_chips(far, 2), up_chips(far, 3)
    arriving = call(arriving_kernel, shaped(MOVING, FACE, HALF), (one, two, three, outgoing, beside))
    arriving_beside = lax.ppermute(arriving, "core", swap)
    eliminated, tiles = call(
        eliminate_kernel,
        (shaped(LINES_HERE, SEGMENT, BLOCK, R), shaped(surfs, 8, HALF)),
        (tile, vector, squares, product, lower, prefixes, carries, arriving, arriving_beside, beside),
        (LISTED, pltpu.VMEM((LINES_HERE, SEGMENT, FACE, R), F32), pltpu.VMEM((2, 8, R), F32)),
        flops=10**9,
        moved=10**7,
    )
    tiles = lax.all_to_all(tiles, SURF, 0, 0, tiled=True)
    tiles = call(merge_kernel, shaped(walls, 8, HALF), (tiles,))
    tiles = lax.all_to_all(tiles, WALL, 0, 0, tiled=True)
    entries = LINES_HERE * SEGMENT * BLOCK * walls * surfs
    return call(
        functools.partial(finish_kernel, entries),
        (shaped(LINES_HERE, SEGMENT, BLOCK, R, dtype=BF16), shaped(2, R)),
        (alive, tiles, vector, eliminated),
        (pltpu.VMEM((LINES_HERE, SEGMENT, BLOCK, R), BF16), pltpu.SemaphoreType.DMA((LINES_HERE,))),
        out_specs=(pl.BlockSpec(memory_space=pl.ANY), in_vmem()),
    )


def solution(mesh):
    split = Mesh(mesh.devices.reshape(4, 2, 4, 8), ("y", "core", "x", "z"))
    placed = (
        P(SURF, WALL, None, None),
        P(SURF),
        P(SURF, None),
        P(SURF, WALL, None, None),
        P(SURF, WALL, None, None, None),
        P(SURF, WALL, None, None),
    )
    return jax.shard_map(
        per_device,
        mesh=split,
        in_specs=placed,
        out_specs=(P(SURF, WALL, None, None), P()),
        check_vma=False,
    )
```

```python
import functools

import jax
import jax.numpy as jnp
from jax import lax
from jax.experimental import pallas as pl
from jax.experimental.pallas import tpu as pltpu
from jax.sharding import Mesh
from jax.sharding import PartitionSpec as P

BLOCK = 320
FACE = 80
LINES_HERE = 4
SEGMENT = 4
MOVING = 3
R = 256
HALF = 128
OWN_MAPS, Y_MAPS = MOVING, MOVING + 1
WALL = ("y", "core")
SURF = ("x", "z")
F32 = jnp.float32
BF16 = jnp.bfloat16
EXACT = lax.Precision.HIGHEST
VMEM = pltpu.VMEM


def in_vmem():
    return pl.BlockSpec(memory_space=VMEM)


class Digits:
    def __init__(self, number, bits):
        self.number, self.bits = number, bits

    def __getitem__(self, at):
        return (self.number >> (self.bits * at)) & ((1 << self.bits) - 1)


def lengths_and_norths(tile):
    return Digits(jnp.max(tile[0:8]).astype(jnp.int32), 6), Digits(jnp.max(tile[8:16]).astype(jnp.int32), 2)


def wall_here():
    return lax.axis_index("y") * 2 + lax.axis_index("core")


def living_here(lengths, line):
    return jnp.clip(lengths[line] - SEGMENT * wall_here(), 0, SEGMENT)


def shortest_line(lengths):
    at = jnp.int32(3)
    for line in (2, 1, 0):
        at = jnp.where(lengths[line] == 1, line, at)
    return at


def line_in_slot(slot, short):
    return jnp.where(slot == MOVING, short, slot + (slot >= short).astype(jnp.int32))


def list_living(lengths, listed, slots=LINES_HERE):
    short = shortest_line(lengths)
    count = jnp.int32(0)
    for slot in range(slots):
        here = living_here(lengths, line_in_slot(slot, short))
        for position in range(SEGMENT):
            listed[count] = slot * SEGMENT + position
            count = count + (position < here).astype(jnp.int32)
    return count


def for_listed(lengths, listed, count, body, together=4):
    short = shortest_line(lengths)

    def one(trip):
        entry = listed[trip]
        slot = entry // SEGMENT
        body(slot, line_in_slot(slot, short), entry % SEGMENT)

    def group(first, size):
        for part in range(size):
            one(first + part)

    whole = count // together

    @pl.loop(0, whole)
    def _(trip):
        group(trip * together, together)

    @pl.loop(whole * together, count)
    def _(trip):
        group(trip, 1)


def wall_face_rows():
    row = lax.broadcasted_iota(jnp.int32, (2 * FACE, BLOCK), 0)
    column = lax.broadcasted_iota(jnp.int32, (2 * FACE, BLOCK), 1)
    second = (row >= FACE).astype(jnp.int32)
    return (column == 4 * (row - FACE * second) + 3 * second).astype(BF16)


def pick(rows, values):
    return jnp.dot(rows, values, preferred_element_type=F32).astype(BF16)


def a_face(block, end):
    return jnp.concatenate([block[64 * v + 16 * end : 64 * v + 16 * end + 16] for v in range(5)], axis=0)


def partial(values):
    return values.reshape(BLOCK // 8, 8, R).sum(axis=0)


def split_exactly(values):
    high = values.astype(BF16)
    low = (values - high.astype(F32)).astype(BF16)
    return high, low


def transposed_times(left, right):
    return lax.dot_general(left, right, (((0,), (0,)), ((), ())), preferred_element_type=F32)


def mapped(matrix, state):
    matrix_high, matrix_low = split_exactly(matrix)
    high, low = split_exactly(state)
    rows = matrix.shape[0]
    both = jnp.dot(jnp.concatenate([matrix_high, matrix_low], axis=0), high, preferred_element_type=F32)
    return both[:rows] + (both[rows:] + jnp.dot(matrix_high, low, preferred_element_type=F32))


def edges_kernel(
    lengths_hbm,
    norths_hbm,
    vector_hbm,
    lifting_hbm,
    inverse_hbm,
    over_core,
    over_y,
    over_pair,
    over_next,
    steps,
    prefixes,
    whole,
    lower,
    inverse,
    vector,
    tile,
    alive,
    lengths,
    norths,
    sems,
    block_sems,
):
    core, odd = lax.axis_index("core"), lax.axis_index("z") % 2
    copies = [
        pltpu.make_async_copy(lengths_hbm, lengths, sems.at[0]),
        pltpu.make_async_copy(norths_hbm, norths, sems.at[1]),
    ]
    for at, position in enumerate((0, SEGMENT - 1)):
        copies.append(
            pltpu.make_async_copy(vector_hbm.at[:, position], vector.at[:, position], block_sems.at[2, at])
        )
    inner = pltpu.make_async_copy(
        vector_hbm.at[:, pl.ds(1, SEGMENT - 2)], vector.at[:, pl.ds(1, SEGMENT - 2)], block_sems.at[2, 2]
    )
    needed = []
    for line in range(LINES_HERE):
        needed.append(pltpu.make_async_copy(inverse_hbm.at[line], inverse.at[line], block_sems.at[0, line]))
        needed.append(pltpu.make_async_copy(lifting_hbm.at[line, :, 0], lower.at[line], block_sems.at[1, line]))
    for copy in copies + [inner] + needed:
        copy.start()
    rows = wall_face_rows()
    for copy in copies:
        copy.wait()
    length_digits, north_digits = jnp.int32(0), jnp.int32(0)
    for line in range(LINES_HERE):
        length_digits = length_digits + (lengths[line] << (6 * line))
        north_digits = north_digits + (norths[0, line] << (2 * line))
    tile[0:8] = jnp.full((8, HALF), length_digits.astype(F32))
    tile[8:16] = jnp.full((8, HALF), north_digits.astype(F32))
    for line in range(LINES_HERE):
        here = living_here(lengths, line)
        for position in range(SEGMENT):
            alive[line, position] = jnp.full((8, HALF), (position < here).astype(jnp.int32).astype(F32))
    short = shortest_line(lengths)
    zero = jnp.zeros((FACE, R), BF16)
    for slot in range(MOVING):
        line = line_in_slot(slot, short)
        here = living_here(lengths, line)
        down = jnp.where(here > 0, pick(rows[:FACE], vector[line, 0]), zero)
        up = jnp.where(here > SEGMENT - 1, pick(rows[FACE:], vector[line, SEGMENT - 1]), zero)
        over_core[slot] = jnp.where(core == 0, up, down)
        over_y[slot] = jnp.where(core == 0, down, up)
    first, last = living_here(lengths, 0), living_here(lengths, LINES_HERE - 1)
    inner.wait()
    for position in range(SEGMENT):
        from_first = jnp.where(position < first, a_face(vector[0, position], 0), zero)
        from_last = jnp.where(position < last, a_face(vector[LINES_HERE - 1, position], 3), zero)
        over_pair[position] = jnp.where(odd == 0, from_last, from_first)
        over_next[position] = jnp.where(odd == 0, from_first, from_last)
    for copy in needed:
        copy.wait()
    lines = [line_in_slot(slot, short) for slot in range(MOVING)]
    so_far = [None] * MOVING
    for position in range(SEGMENT):
        for slot, line in enumerate(lines):
            step = lax.dot_general(
                inverse[line, position],
                lower[line, position],
                (((1,), (1,)), ((), ())),
                preferred_element_type=F32,
            )
            steps[slot, position] = jnp.where(position < living_here(lengths, line), -step, 0.0)
    for position in range(SEGMENT):
        for slot in range(MOVING):
            step = steps[slot, position]
            so_far[slot] = step if position == 0 else mapped(step, so_far[slot])
            if position < SEGMENT - 1:
                prefixes[slot, position] = so_far[slot]
    whole[...] = jnp.concatenate(so_far + [jnp.zeros((FACE, R - MOVING * FACE), F32)], axis=1)


def diagonal_kernel(tile, vector, diagonal_hbm, product, traces, squares, diagonal, sems, wide):
    def block_copy(line):
        return pltpu.make_async_copy(diagonal_hbm.at[line], diagonal.at[line], sems.at[line])

    for line in range(LINES_HERE):
        block_copy(line).start()
    lengths, _ = lengths_and_norths(tile)
    for line in range(LINES_HERE):
        here = living_here(lengths, line)
        for position in range(SEGMENT):

            @pl.when(position >= here)
            def _():
                traces[line, position] = jnp.zeros((6, FACE, R), BF16)

    squares[...] = jnp.zeros_like(squares)

    def body(line, position):
        values = vector[line, position]
        product[line, position] = jnp.dot(diagonal[line, position], values, preferred_element_type=F32)
        whole = values.astype(F32)
        squares[...] += partial(whole * whole)
        for half in range(2):
            columns = slice(half * HALF, (half + 1) * HALF)
            wide[half] = whole[:, columns]
            for face, first in ((0, 0), (1, 3)):
                traces[line, position, face, :, columns] = wide[half, pl.ds(first, FACE, stride=4), :].astype(BF16)
        traces[line, position, 2] = a_face(values, 0)
        traces[line, position, 3] = a_face(values, 3)
        runs = whole.reshape(10, 4, 8, R)
        upper = lax.broadcasted_iota(jnp.int32, (10, 8, R), 1) < 4
        south = jnp.where(upper, runs[:, 0], pltpu.roll(runs[:, 2], 4, axis=1))
        north = jnp.where(upper, pltpu.roll(runs[:, 1], 4, axis=1), runs[:, 3])
        traces[line, position, 4] = south.reshape(FACE, R).astype(BF16)
        traces[line, position, 5] = north.reshape(FACE, R).astype(BF16)

    @pl.loop(0, LINES_HERE)
    def _(line):
        here = living_here(lengths, line)
        block_copy(line).wait()

        @pl.when(here == SEGMENT)
        def _():
            for position in range(SEGMENT):
                body(line, position)

        @pl.when(here < SEGMENT)
        def _():
            @pl.loop(0, here)
            def _(position):
                body(line, position)


def product_kernel(
    tile,
    traces,
    over_core,
    over_y,
    over_pair,
    over_next,
    lifting,
    inverse,
    steps,
    map_here,
    map_y,
    product_in,
    product,
    carries,
    outgoing,
    listed,
    driven,
):
    core, odd = lax.axis_index("core"), lax.axis_index("z") % 2
    lengths, norths = lengths_and_norths(tile)
    zero = jnp.zeros((FACE, R), BF16)

    def multiply(slot, line, position):
        wall_slot = jnp.minimum(slot, MOVING - 1)
        moving = slot < MOVING
        from_core = jnp.where(moving, over_core[wall_slot], zero)
        from_y = jnp.where(moving, over_y[wall_slot], zero)
        below_edge = jnp.where(core == 0, from_y, from_core)
        above_edge = jnp.where(core == 0, from_core, from_y)
        below = jnp.where(position == 0, below_edge, traces[line, jnp.maximum(position - 1, 0), 1])
        above = jnp.where(
            position == SEGMENT - 1, above_edge, traces[line, jnp.minimum(position + 1, SEGMENT - 1), 0]
        )
        west_edge = jnp.where(odd == 0, over_next[position], over_pair[position])
        east_edge = jnp.where(odd == 0, over_pair[position], over_next[position])
        west = jnp.where(line == 0, west_edge, traces[jnp.maximum(line - 1, 0), position, 3])
        east = jnp.where(
            line == LINES_HERE - 1, east_edge, traces[jnp.minimum(line + 1, LINES_HERE - 1), position, 2]
        )
        north_line = norths[line]
        south_line = jnp.int32(0)
        for other in range(1, LINES_HERE):
            south_line = jnp.where(norths[other] == line, other, south_line)
        south = traces[south_line, position, 5]
        north = traces[north_line, position, 4]
        neighbours = jnp.concatenate([below, above, west, east, south, north], axis=0)
        blocks = lifting[line, position].reshape(6 * FACE, BLOCK)
        product[line, position] = product_in[line, position] + transposed_times(blocks, neighbours)

    count = list_living(lengths, listed)
    for_listed(lengths, listed, count, multiply)

    for slot in range(MOVING):
        for position in range(SEGMENT):

            @pl.when(position >= living_here(lengths, line_in_slot(slot, shortest_line(lengths))))
            def _():
                driven[slot, position] = jnp.zeros((FACE, R), F32)

    def drive(slot, line, position):
        high, low = split_exactly(product[line, position])
        rows = inverse[line, position]
        tail = rows[:, 256:]
        driven[slot, position] = jnp.dot(
            jnp.concatenate([rows[:, :256], rows[:, :256], tail, tail], axis=1),
            jnp.concatenate([high[:256], low[:256], high[256:], low[256:]], axis=0),
            preferred_element_type=F32,
        )

    for_listed(lengths, listed, list_living(lengths, listed, MOVING), drive)
    carried = [driven[slot, 0] for slot in range(MOVING)]
    for position in range(1, SEGMENT):
        for slot in range(MOVING):
            carries[slot, position - 1] = carried[slot]
            carried[slot] = driven[slot, position] + mapped(steps[slot, position], carried[slot])
    for slot in range(MOVING):
        outgoing[slot] = carried[slot]
    outgoing[OWN_MAPS] = map_here[...]
    outgoing[Y_MAPS] = map_y[...]


def map_of(maps, slot):
    return maps[:, slot * FACE : (slot + 1) * FACE]


def chip_kernel(mine, other, near, far):
    core, y = lax.axis_index("core"), lax.axis_index("y")
    second_maps = jnp.where(core == 0, other[OWN_MAPS], mine[OWN_MAPS])
    values = []
    for slot in range(MOVING):
        own, away = mine[slot], other[slot]
        first_value = jnp.where(core == 0, own[:, :HALF], away[:, HALF:])
        second_value = jnp.where(core == 0, away[:, :HALF], own[:, HALF:])
        values.append(mapped(map_of(second_maps, slot), first_value) + second_value)
    for slot in range(MOVING):
        near[slot] = values[slot]
        far[slot] = values[slot]

    @pl.when(y == 0)
    def _():
        through_chip(mine, other, values, far)


def through_chip(mine, other, values, results):
    core = lax.axis_index("core")
    first_maps = jnp.where(core == 0, mine[Y_MAPS], other[Y_MAPS])
    second_maps = jnp.where(core == 0, other[Y_MAPS], mine[Y_MAPS])
    moved = [mapped(map_of(first_maps, slot), value) for slot, value in enumerate(values)]
    for slot, value in enumerate(moved):
        results[slot] = mapped(map_of(second_maps, slot), value)


def arriving_kernel(one, two, three, mine, other, arriving):
    y = lax.axis_index("y")
    below = [two[slot] + three[slot] for slot in range(MOVING)]
    for slot in range(MOVING):
        arriving[slot] = below[slot]

    @pl.when(y == 3)
    def _():
        through_chip(mine, other, below, arriving)

    for slot in range(MOVING):
        arriving[slot] = arriving[slot] + one[slot]


def eliminate_kernel(
    tile,
    vector,
    squares,
    product,
    lower,
    prefixes,
    carries,
    mine,
    other,
    beside,
    eliminated,
    tiles,
    listed,
    entering,
    sums,
):
    core = lax.axis_index("core")
    lengths, _ = lengths_and_norths(tile)
    entering[...] = jnp.zeros_like(entering)
    values = []
    for slot in range(MOVING):
        left = jnp.where(core == 0, mine[slot], other[slot])
        right = jnp.where(core == 0, other[slot], mine[slot])
        value = jnp.concatenate([left, right], axis=1)
        passed = mapped(map_of(beside[OWN_MAPS], slot), value) + beside[slot]
        values.append(jnp.where(core == 0, value, passed))
    for slot, value in enumerate(values):
        entering[slot, 0] = value
        moved = mapped(prefixes[slot].reshape((SEGMENT - 1) * FACE, FACE), value)
        for position in range(1, SEGMENT):
            entering[slot, position] = carries[slot, position - 1] + moved[(position - 1) * FACE : position * FACE]

    count = list_living(lengths, listed)
    sums[...] = jnp.zeros_like(sums)

    def correct(slot, line, position):
        high, low = split_exactly(entering[slot, position])
        block = lower[line, position]
        correction = transposed_times(jnp.concatenate([block, block], axis=0), jnp.concatenate([high, low], axis=0))
        value = product[line, position] - correction
        eliminated[line, position] = value
        masked = vector[line, position].astype(F32)
        sums[0] += partial(masked * value)

    for_listed(lengths, listed, count, correct)
    cross = sums[0].sum(axis=0, keepdims=True)
    square = squares[...].sum(axis=0, keepdims=True)
    share = jnp.where(square > 0, cross / square, 0.0)

    def leave(slot, line, position):
        rest = eliminated[line, position] - share * vector[line, position].astype(F32)
        sums[1] += partial(rest * rest)

    for_listed(lengths, listed, count, leave)
    rest = sums[1].sum(axis=0, keepdims=True)
    pieces = [part[:, at : at + HALF] for part in (cross, square, rest) for at in (0, HALF)]
    sums_tile = jnp.concatenate(pieces + [jnp.zeros((2, HALF), F32)], axis=0)
    for copy in range(tiles.shape[0]):
        tiles[copy] = sums_tile


def merged(tiles):
    cross, square, rest = tiles[:, 0:2], tiles[:, 2:4], tiles[:, 4:6]
    all_cross, all_square = cross.sum(axis=0), square.sum(axis=0)
    own = jnp.where(square > 0, cross / square, 0.0)
    ratio = all_cross / all_square
    away = jnp.where(square > 0, own - ratio[None], 0.0)
    all_rest = (rest + (square * away) * away).sum(axis=0)
    return all_cross, all_square, all_rest, ratio


def merge_kernel(tiles_in, tiles):
    cross, square, rest, _ = merged(tiles_in[...])
    tile = jnp.concatenate([cross, square, rest, jnp.zeros((2, HALF), F32)], axis=0)
    for copy in range(tiles.shape[0]):
        tiles[copy] = tile


def finish_kernel(entries, alive, tiles, vector, eliminated, basis, coefs, held, sems):
    _, _, rest, ratio = merged(tiles[...])
    spread = jnp.sqrt(rest / entries + 1e-06)
    ratio = jnp.concatenate([ratio[0:1], ratio[1:2]], axis=1)
    spread = jnp.concatenate([spread[0:1], spread[1:2]], axis=1)
    coefs[...] = jnp.concatenate([ratio, spread], axis=0)
    scale = 1.0 / spread
    copies = []
    for line in range(LINES_HERE):
        for position in range(SEGMENT):
            masked = vector[line, position].astype(F32)
            value = (eliminated[line, position] - ratio * masked) * scale
            flags = alive[line, position]
            flags = jnp.concatenate([flags, flags], axis=1) > 0
            value = jnp.where(flags[None], value.reshape(BLOCK // 8, 8, R), 0.0)
            held[line, position] = value.reshape(BLOCK, R).astype(BF16)
        copy = pltpu.make_async_copy(held.at[line], basis.at[line], sems.at[line])
        copy.start()
        copies.append(copy)
    for copy in copies:
        copy.wait()


def call(kernel, outs, ins, scratch=(), limit=12, flops=0, moved=0, out_specs=None, in_hbm=()):
    return pl.pallas_call(
        kernel,
        out_shape=outs,
        in_specs=[
            pl.BlockSpec(memory_space=pltpu.HBM) if at in in_hbm else in_vmem()
            for at, arg in enumerate(ins)
        ],
        out_specs=out_specs or jax.tree.map(lambda _: in_vmem(), outs),
        scratch_shapes=list(scratch),
        compiler_params=pltpu.CompilerParams(vmem_limit_bytes=limit * 2**20),
        cost_estimate=pl.CostEstimate(flops=flops, bytes_accessed=moved, transcendentals=0),
        name=getattr(kernel, "__name__", "finish_kernel"),
    )(*[pltpu.with_memory_space_constraint(arg, pltpu.HBM) if at in in_hbm else arg for at, arg in enumerate(ins)])


def shaped(*shape, dtype=F32):
    return jax.ShapeDtypeStruct(shape, dtype)


LISTED = pltpu.SMEM((LINES_HERE * SEGMENT + 1,), jnp.int32)


def per_device(vector, lengths, north_of, diagonal, lifting, inverse_rows):
    edge = shaped(MOVING, FACE, R, dtype=BF16)
    side = shaped(SEGMENT, FACE, R, dtype=BF16)
    blocks = shaped(LINES_HERE, SEGMENT, FACE, BLOCK, dtype=BF16)
    over_core, over_y, over_pair, over_next, steps, prefixes, whole, lower, inverse, vector, tile, alive = call(
        edges_kernel,
        (
            edge,
            edge,
            side,
            side,
            shaped(MOVING, SEGMENT, FACE, FACE),
            shaped(MOVING, SEGMENT - 1, FACE, FACE),
            shaped(FACE, R),
            blocks,
            blocks,
            shaped(LINES_HERE, SEGMENT, BLOCK, R, dtype=BF16),
            shaped(16, HALF),
            shaped(LINES_HERE, SEGMENT, 8, HALF),
        ),
        (lengths, north_of, vector, lifting, inverse_rows),
        (
            pltpu.SMEM((LINES_HERE,), jnp.int32),
            pltpu.SMEM((1, LINES_HERE), jnp.int32),
            pltpu.SemaphoreType.DMA((2,)),
            pltpu.SemaphoreType.DMA((3, LINES_HERE)),
        ),
        in_hbm=(0, 1, 2, 3, 4),
    )
    walls, surfs = lax.axis_size(WALL), lax.axis_size(SURF)
    swap = [(0, 1), (1, 0)]
    over_core = lax.ppermute(over_core, "core", swap)
    rungs = [(i, i + 1) for i in range(1, walls - 1, 2)]
    over_y = lax.ppermute(over_y, WALL, rungs + [(b, a) for a, b in rungs])
    over_pair = lax.ppermute(over_pair, SURF, [(i, i ^ 1) for i in range(surfs)])
    nexts = [(i, (i + 1) % surfs) for i in range(1, surfs, 2)]
    over_next = lax.ppermute(over_next, SURF, nexts + [(b, a) for a, b in nexts])

    map_y = lax.ppermute(whole, "y", [(1, 0), (2, 3)])
    product, traces, squares = call(
        diagonal_kernel,
        (
            shaped(LINES_HERE, SEGMENT, BLOCK, R),
            shaped(LINES_HERE, SEGMENT, 6, FACE, R, dtype=BF16),
            shaped(8, R),
        ),
        (tile, vector, diagonal),
        (
            pltpu.VMEM((LINES_HERE, SEGMENT, BLOCK, BLOCK), BF16),
            pltpu.SemaphoreType.DMA((LINES_HERE,)),
            pltpu.VMEM((2, BLOCK, HALF), F32),
        ),
        in_hbm=(2,),
    )
    product, carries, outgoing = call(
        product_kernel,
        (
            shaped(LINES_HERE, SEGMENT, BLOCK, R),
            shaped(MOVING, SEGMENT - 1, FACE, R),
            shaped(MOVING + 2, FACE, R),
        ),
        (
            tile,
            traces,
            over_core,
            over_y,
            over_pair,
            over_next,
            lifting,
            inverse,
            steps,
            whole,
            map_y,
            product,
        ),
        (LISTED, pltpu.VMEM((LINES_HERE, SEGMENT, FACE, R), F32)),
    )
    ranks = lax.axis_size("y")

    def up_chips(value, far):
        return lax.ppermute(value, "y", [(i, i + far) for i in range(ranks - far)])

    beside = lax.ppermute(outgoing, "core", swap)
    near, far = call(chip_kernel, (shaped(MOVING, FACE, HALF), shaped(MOVING, FACE, HALF)), (outgoing, beside))
    one, two, three = up_chips(near, 1), up_chips(far, 2), up_chips(far, 3)
    arriving = call(arriving_kernel, shaped(MOVING, FACE, HALF), (one, two, three, outgoing, beside))
    arriving_beside = lax.ppermute(arriving, "core", swap)
    eliminated, tiles = call(
        eliminate_kernel,
        (shaped(LINES_HERE, SEGMENT, BLOCK, R), shaped(surfs, 8, HALF)),
        (tile, vector, squares, product, lower, prefixes, carries, arriving, arriving_beside, beside),
        (LISTED, pltpu.VMEM((LINES_HERE, SEGMENT, FACE, R), F32), pltpu.VMEM((2, 8, R), F32)),
        flops=10**9,
        moved=10**7,
    )
    tiles = lax.all_to_all(tiles, SURF, 0, 0, tiled=True)
    tiles = call(merge_kernel, shaped(walls, 8, HALF), (tiles,))
    tiles = lax.all_to_all(tiles, WALL, 0, 0, tiled=True)
    entries = LINES_HERE * SEGMENT * BLOCK * walls * surfs
    return call(
        functools.partial(finish_kernel, entries),
        (shaped(LINES_HERE, SEGMENT, BLOCK, R, dtype=BF16), shaped(2, R)),
        (alive, tiles, vector, eliminated),
        (pltpu.VMEM((LINES_HERE, SEGMENT, BLOCK, R), BF16), pltpu.SemaphoreType.DMA((LINES_HERE,))),
        out_specs=(pl.BlockSpec(memory_space=pl.ANY), in_vmem()),
    )


def solution(mesh):
    split = Mesh(mesh.devices.reshape(4, 2, 4, 8), ("y", "core", "x", "z"))
    placed = (
        P(SURF, WALL, None, None),
        P(SURF),
        P(SURF, None),
        P(SURF, WALL, None, None),
        P(SURF, WALL, None, None, None),
        P(SURF, WALL, None, None),
    )
    return jax.shard_map(
        per_device,
        mesh=split,
        in_specs=placed,
        out_specs=(P(SURF, WALL, None, None), P()),
        check_vma=False,
    )
```

```python
import functools

import jax
import jax.numpy as jnp
from jax import lax
from jax.experimental import pallas as pl
from jax.experimental.pallas import tpu as pltpu
from jax.sharding import Mesh
from jax.sharding import PartitionSpec as P

BLOCK = 320
FACE = 80
LINES_HERE = 4
SEGMENT = 4
MOVING = 3
R = 256
HALF = 128
OWN_MAPS, Y_MAPS = MOVING, MOVING + 1
WALL = ("y", "core")
SURF = ("x", "z")
F32 = jnp.float32
BF16 = jnp.bfloat16
EXACT = lax.Precision.HIGHEST
VMEM = pltpu.VMEM


def in_vmem():
    return pl.BlockSpec(memory_space=VMEM)


class Digits:
    def __init__(self, number, bits):
        self.number, self.bits = number, bits

    def __getitem__(self, at):
        return (self.number >> (self.bits * at)) & ((1 << self.bits) - 1)


def lengths_and_norths(tile):
    return Digits(jnp.max(tile[0:8]).astype(jnp.int32), 6), Digits(jnp.max(tile[8:16]).astype(jnp.int32), 2)


def wall_here():
    return lax.axis_index("y") * 2 + lax.axis_index("core")


def living_here(lengths, line):
    return jnp.clip(lengths[line] - SEGMENT * wall_here(), 0, SEGMENT)


def shortest_line(lengths):
    at = jnp.int32(3)
    for line in (2, 1, 0):
        at = jnp.where(lengths[line] == 1, line, at)
    return at


def line_in_slot(slot, short):
    return jnp.where(slot == MOVING, short, slot + (slot >= short).astype(jnp.int32))


def list_living(lengths, listed, slots=LINES_HERE):
    short = shortest_line(lengths)
    count = jnp.int32(0)
    for slot in range(slots):
        here = living_here(lengths, line_in_slot(slot, short))
        for position in range(SEGMENT):
            listed[count] = slot * SEGMENT + position
            count = count + (position < here).astype(jnp.int32)
    return count


def for_listed(lengths, listed, count, body, together=4):
    short = shortest_line(lengths)

    def one(trip):
        entry = listed[trip]
        slot = entry // SEGMENT
        body(slot, line_in_slot(slot, short), entry % SEGMENT)

    def group(first, size):
        for part in range(size):
            one(first + part)

    whole = count // together

    @pl.loop(0, whole)
    def _(trip):
        group(trip * together, together)

    @pl.loop(whole * together, count)
    def _(trip):
        group(trip, 1)


def wall_face_rows():
    row = lax.broadcasted_iota(jnp.int32, (2 * FACE, BLOCK), 0)
    column = lax.broadcasted_iota(jnp.int32, (2 * FACE, BLOCK), 1)
    second = (row >= FACE).astype(jnp.int32)
    return (column == 4 * (row - FACE * second) + 3 * second).astype(BF16)


def pick(rows, values):
    return jnp.dot(rows, values, preferred_element_type=F32).astype(BF16)


def a_face(block, end):
    return jnp.concatenate([block[64 * v + 16 * end : 64 * v + 16 * end + 16] for v in range(5)], axis=0)


def partial(values):
    return values.reshape(BLOCK // 8, 8, R).sum(axis=0)


def split_exactly(values):
    high = values.astype(BF16)
    low = (values - high.astype(F32)).astype(BF16)
    return high, low


def transposed_times(left, right):
    return lax.dot_general(left, right, (((0,), (0,)), ((), ())), preferred_element_type=F32)


def mapped(matrix, state):
    matrix_high, matrix_low = split_exactly(matrix)
    high, low = split_exactly(state)
    rows = matrix.shape[0]
    both = jnp.dot(jnp.concatenate([matrix_high, matrix_low], axis=0), high, preferred_element_type=F32)
    return both[:rows] + (both[rows:] + jnp.dot(matrix_high, low, preferred_element_type=F32))


def edges_kernel(
    lengths_hbm,
    norths_hbm,
    vector_hbm,
    lifting_hbm,
    inverse_hbm,
    over_core,
    over_y,
    over_pair,
    over_next,
    steps,
    prefixes,
    last_two,
    whole,
    lower,
    inverse,
    vector,
    tile,
    alive,
    lengths,
    norths,
    sems,
    block_sems,
):
    core, odd = lax.axis_index("core"), lax.axis_index("z") % 2
    copies = [
        pltpu.make_async_copy(lengths_hbm, lengths, sems.at[0]),
        pltpu.make_async_copy(norths_hbm, norths, sems.at[1]),
    ]
    for at, position in enumerate((0, SEGMENT - 1)):
        copies.append(
            pltpu.make_async_copy(vector_hbm.at[:, position], vector.at[:, position], block_sems.at[2, at])
        )
    inner = pltpu.make_async_copy(
        vector_hbm.at[:, pl.ds(1, SEGMENT - 2)], vector.at[:, pl.ds(1, SEGMENT - 2)], block_sems.at[2, 2]
    )
    needed = []
    for line in range(LINES_HERE):
        needed.append(pltpu.make_async_copy(inverse_hbm.at[line], inverse.at[line], block_sems.at[0, line]))
        needed.append(pltpu.make_async_copy(lifting_hbm.at[line, :, 0], lower.at[line], block_sems.at[1, line]))
    for copy in copies + [inner] + needed:
        copy.start()
    rows = wall_face_rows()
    for copy in copies:
        copy.wait()
    length_digits, north_digits = jnp.int32(0), jnp.int32(0)
    for line in range(LINES_HERE):
        length_digits = length_digits + (lengths[line] << (6 * line))
        north_digits = north_digits + (norths[0, line] << (2 * line))
    tile[0:8] = jnp.full((8, HALF), length_digits.astype(F32))
    tile[8:16] = jnp.full((8, HALF), north_digits.astype(F32))
    for line in range(LINES_HERE):
        here = living_here(lengths, line)
        for position in range(SEGMENT):
            alive[line, position] = jnp.full((8, HALF), (position < here).astype(jnp.int32).astype(F32))
    short = shortest_line(lengths)
    zero = jnp.zeros((FACE, R), BF16)
    for slot in range(MOVING):
        line = line_in_slot(slot, short)
        here = living_here(lengths, line)
        down = jnp.where(here > 0, pick(rows[:FACE], vector[line, 0]), zero)
        up = jnp.where(here > SEGMENT - 1, pick(rows[FACE:], vector[line, SEGMENT - 1]), zero)
        over_core[slot] = jnp.where(core == 0, up, down)
        over_y[slot] = jnp.where(core == 0, down, up)
    first, last = living_here(lengths, 0), living_here(lengths, LINES_HERE - 1)
    inner.wait()
    for position in range(SEGMENT):
        from_first = jnp.where(position < first, a_face(vector[0, position], 0), zero)
        from_last = jnp.where(position < last, a_face(vector[LINES_HERE - 1, position], 3), zero)
        over_pair[position] = jnp.where(odd == 0, from_last, from_first)
        over_next[position] = jnp.where(odd == 0, from_first, from_last)
    for copy in needed:
        copy.wait()
    lines = [line_in_slot(slot, short) for slot in range(MOVING)]
    for position in range(SEGMENT):
        for slot, line in enumerate(lines):
            step = lax.dot_general(
                inverse[line, position],
                lower[line, position],
                (((1,), (1,)), ((), ())),
                preferred_element_type=F32,
            )
            steps[slot, position] = jnp.where(position < living_here(lengths, line), -step, 0.0)
    for slot in range(MOVING):
        prefixes[slot, 0] = steps[slot, 0]
        prefixes[slot, 1] = mapped(steps[slot, 1], steps[slot, 0])
        last_two[slot] = mapped(steps[slot, 3], steps[slot, 2])
    so_far = []
    for slot in range(MOVING):
        prefixes[slot, 2] = mapped(steps[slot, 2], prefixes[slot, 1])
        so_far.append(mapped(last_two[slot], prefixes[slot, 1]))
    whole[...] = jnp.concatenate(so_far + [jnp.zeros((FACE, R - MOVING * FACE), F32)], axis=1)


def diagonal_kernel(tile, vector, diagonal, product, traces, squares, listed, wide):
    lengths, _ = lengths_and_norths(tile)
    for line in range(LINES_HERE):
        here = living_here(lengths, line)
        for position in range(SEGMENT):

            @pl.when(position >= here)
            def _():
                traces[line, position] = jnp.zeros((6, FACE, R), BF16)

    squares[...] = jnp.zeros_like(squares)

    def body(slot, line, position):
        values = vector[line, position]
        product[line, position] = jnp.dot(diagonal[line, position], values, preferred_element_type=F32)
        whole = values.astype(F32)
        squares[...] += partial(whole * whole)
        for half in range(2):
            columns = slice(half * HALF, (half + 1) * HALF)
            wide[half] = whole[:, columns]
            for face, first in ((0, 0), (1, 3)):
                traces[line, position, face, :, columns] = wide[half, pl.ds(first, FACE, stride=4), :].astype(BF16)
        traces[line, position, 2] = a_face(values, 0)
        traces[line, position, 3] = a_face(values, 3)
        runs = whole.reshape(10, 4, 8, R)
        upper = lax.broadcasted_iota(jnp.int32, (10, 8, R), 1) < 4
        south = jnp.where(upper, runs[:, 0], pltpu.roll(runs[:, 2], 4, axis=1))
        north = jnp.where(upper, pltpu.roll(runs[:, 1], 4, axis=1), runs[:, 3])
        traces[line, position, 4] = south.reshape(FACE, R).astype(BF16)
        traces[line, position, 5] = north.reshape(FACE, R).astype(BF16)

    for_listed(lengths, listed, list_living(lengths, listed), body)


def product_kernel(
    tile,
    traces,
    over_core,
    over_y,
    over_pair,
    over_next,
    lifting,
    inverse,
    steps,
    last_two,
    map_here,
    map_y,
    product_in,
    product,
    carries,
    outgoing,
    listed,
    driven,
):
    core, odd = lax.axis_index("core"), lax.axis_index("z") % 2
    lengths, norths = lengths_and_norths(tile)
    zero = jnp.zeros((FACE, R), BF16)

    def multiply(slot, line, position):
        wall_slot = jnp.minimum(slot, MOVING - 1)
        moving = slot < MOVING
        from_core = jnp.where(moving, over_core[wall_slot], zero)
        from_y = jnp.where(moving, over_y[wall_slot], zero)
        below_edge = jnp.where(core == 0, from_y, from_core)
        above_edge = jnp.where(core == 0, from_core, from_y)
        below = jnp.where(position == 0, below_edge, traces[line, jnp.maximum(position - 1, 0), 1])
        above = jnp.where(
            position == SEGMENT - 1, above_edge, traces[line, jnp.minimum(position + 1, SEGMENT - 1), 0]
        )
        west_edge = jnp.where(odd == 0, over_next[position], over_pair[position])
        east_edge = jnp.where(odd == 0, over_pair[position], over_next[position])
        west = jnp.where(line == 0, west_edge, traces[jnp.maximum(line - 1, 0), position, 3])
        east = jnp.where(
            line == LINES_HERE - 1, east_edge, traces[jnp.minimum(line + 1, LINES_HERE - 1), position, 2]
        )
        north_line = norths[line]
        south_line = jnp.int32(0)
        for other in range(1, LINES_HERE):
            south_line = jnp.where(norths[other] == line, other, south_line)
        south = traces[south_line, position, 5]
        north = traces[north_line, position, 4]
        neighbours = jnp.concatenate([below, above, west, east, south, north], axis=0)
        blocks = lifting[line, position].reshape(6 * FACE, BLOCK)
        product[line, position] = product_in[line, position] + transposed_times(blocks, neighbours)

    count = list_living(lengths, listed)
    for_listed(lengths, listed, count, multiply)

    for slot in range(MOVING):
        for position in range(SEGMENT):

            @pl.when(position >= living_here(lengths, line_in_slot(slot, shortest_line(lengths))))
            def _():
                driven[slot, position] = jnp.zeros((FACE, R), F32)

    def drive(slot, line, position):
        high, low = split_exactly(product[line, position])
        rows = inverse[line, position]
        tail = rows[:, 256:]
        driven[slot, position] = jnp.dot(
            jnp.concatenate([rows[:, :256], rows[:, :256], tail, tail], axis=1),
            jnp.concatenate([high[:256], low[:256], high[256:], low[256:]], axis=0),
            preferred_element_type=F32,
        )

    for_listed(lengths, listed, list_living(lengths, listed, MOVING), drive)
    for slot in range(MOVING):
        carries[slot, 0] = driven[slot, 0]
        carries[slot, 1] = driven[slot, 1] + mapped(steps[slot, 1], driven[slot, 0])
        outgoing[slot] = driven[slot, 3] + mapped(steps[slot, 3], driven[slot, 2])
    for slot in range(MOVING):
        carries[slot, 2] = driven[slot, 2] + mapped(steps[slot, 2], carries[slot, 1])
        outgoing[slot] += mapped(last_two[slot], carries[slot, 1])
    outgoing[OWN_MAPS] = map_here[...]
    outgoing[Y_MAPS] = map_y[...]


def map_of(maps, slot):
    return maps[:, slot * FACE : (slot + 1) * FACE]


def chip_kernel(mine, other, near, far):
    core, y = lax.axis_index("core"), lax.axis_index("y")
    second_maps = jnp.where(core == 0, other[OWN_MAPS], mine[OWN_MAPS])
    values = []
    for slot in range(MOVING):
        own, away = mine[slot], other[slot]
        first_value = jnp.where(core == 0, own[:, :HALF], away[:, HALF:])
        second_value = jnp.where(core == 0, away[:, :HALF], own[:, HALF:])
        values.append(mapped(map_of(second_maps, slot), first_value) + second_value)
    for slot in range(MOVING):
        near[slot] = values[slot]
        far[slot] = values[slot]

    @pl.when(y == 0)
    def _():
        through_chip(mine, other, values, far)


def through_chip(mine, other, values, results):
    core = lax.axis_index("core")
    first_maps = jnp.where(core == 0, mine[Y_MAPS], other[Y_MAPS])
    second_maps = jnp.where(core == 0, other[Y_MAPS], mine[Y_MAPS])
    moved = [mapped(map_of(first_maps, slot), value) for slot, value in enumerate(values)]
    for slot, value in enumerate(moved):
        results[slot] = mapped(map_of(second_maps, slot), value)


def arriving_kernel(one, two, three, mine, other, arriving):
    y = lax.axis_index("y")
    below = [two[slot] + three[slot] for slot in range(MOVING)]
    for slot in range(MOVING):
        arriving[slot] = below[slot]

    @pl.when(y == 3)
    def _():
        through_chip(mine, other, below, arriving)

    for slot in range(MOVING):
        arriving[slot] = arriving[slot] + one[slot]


def eliminate_kernel(
    tile,
    vector,
    squares,
    product,
    lower,
    prefixes,
    carries,
    mine,
    other,
    beside,
    eliminated,
    tiles,
    listed,
    entering,
    sums,
):
    core = lax.axis_index("core")
    lengths, _ = lengths_and_norths(tile)
    entering[...] = jnp.zeros_like(entering)
    values = []
    for slot in range(MOVING):
        left = jnp.where(core == 0, mine[slot], other[slot])
        right = jnp.where(core == 0, other[slot], mine[slot])
        value = jnp.concatenate([left, right], axis=1)
        passed = mapped(map_of(beside[OWN_MAPS], slot), value) + beside[slot]
        values.append(jnp.where(core == 0, value, passed))
    for slot, value in enumerate(values):
        entering[slot, 0] = value
        moved = mapped(prefixes[slot].reshape((SEGMENT - 1) * FACE, FACE), value)
        for position in range(1, SEGMENT):
            entering[slot, position] = carries[slot, position - 1] + moved[(position - 1) * FACE : position * FACE]

    count = list_living(lengths, listed)
    sums[...] = jnp.zeros_like(sums)

    def correct(slot, line, position):
        high, low = split_exactly(entering[slot, position])
        block = lower[line, position]
        correction = transposed_times(jnp.concatenate([block, block], axis=0), jnp.concatenate([high, low], axis=0))
        value = product[line, position] - correction
        eliminated[line, position] = value
        masked = vector[line, position].astype(F32)
        sums[0] += partial(masked * value)

    for_listed(lengths, listed, count, correct)
    cross = sums[0].sum(axis=0, keepdims=True)
    square = squares[...].sum(axis=0, keepdims=True)
    share = jnp.where(square > 0, cross / square, 0.0)

    def leave(slot, line, position):
        rest = eliminated[line, position] - share * vector[line, position].astype(F32)
        sums[1] += partial(rest * rest)

    for_listed(lengths, listed, count, leave)
    rest = sums[1].sum(axis=0, keepdims=True)
    pieces = [part[:, at : at + HALF] for part in (cross, square, rest) for at in (0, HALF)]
    sums_tile = jnp.concatenate(pieces + [jnp.zeros((2, HALF), F32)], axis=0)
    for copy in range(tiles.shape[0]):
        tiles[copy] = sums_tile


def merged(tiles):
    cross, square, rest = tiles[:, 0:2], tiles[:, 2:4], tiles[:, 4:6]
    all_cross, all_square = cross.sum(axis=0), square.sum(axis=0)
    own = jnp.where(square > 0, cross / square, 0.0)
    ratio = all_cross / all_square
    away = jnp.where(square > 0, own - ratio[None], 0.0)
    all_rest = (rest + (square * away) * away).sum(axis=0)
    return all_cross, all_square, all_rest, ratio


def merge_kernel(tiles_in, tiles):
    cross, square, rest, _ = merged(tiles_in[...])
    tile = jnp.concatenate([cross, square, rest, jnp.zeros((2, HALF), F32)], axis=0)
    for copy in range(tiles.shape[0]):
        tiles[copy] = tile


def finish_kernel(entries, alive, tiles, vector, eliminated, basis, coefs, held, sems):
    _, _, rest, ratio = merged(tiles[...])
    spread = jnp.sqrt(rest / entries + 1e-06)
    ratio = jnp.concatenate([ratio[0:1], ratio[1:2]], axis=1)
    spread = jnp.concatenate([spread[0:1], spread[1:2]], axis=1)
    coefs[...] = jnp.concatenate([ratio, spread], axis=0)
    scale = 1.0 / spread
    copies = []
    for line in range(LINES_HERE):
        for position in range(SEGMENT):
            masked = vector[line, position].astype(F32)
            value = (eliminated[line, position] - ratio * masked) * scale
            flags = alive[line, position]
            flags = jnp.concatenate([flags, flags], axis=1) > 0
            value = jnp.where(flags[None], value.reshape(BLOCK // 8, 8, R), 0.0)
            held[line, position] = value.reshape(BLOCK, R).astype(BF16)
        copy = pltpu.make_async_copy(held.at[line], basis.at[line], sems.at[line])
        copy.start()
        copies.append(copy)
    for copy in copies:
        copy.wait()


def call(kernel, outs, ins, scratch=(), limit=12, flops=0, moved=0, out_specs=None, in_hbm=()):
    return pl.pallas_call(
        kernel,
        out_shape=outs,
        in_specs=[
            pl.BlockSpec(memory_space=pltpu.HBM) if at in in_hbm else in_vmem()
            for at, arg in enumerate(ins)
        ],
        out_specs=out_specs or jax.tree.map(lambda _: in_vmem(), outs),
        scratch_shapes=list(scratch),
        compiler_params=pltpu.CompilerParams(vmem_limit_bytes=limit * 2**20),
        cost_estimate=pl.CostEstimate(flops=flops, bytes_accessed=moved, transcendentals=0),
        name=getattr(kernel, "__name__", "finish_kernel"),
    )(*[pltpu.with_memory_space_constraint(arg, pltpu.HBM) if at in in_hbm else arg for at, arg in enumerate(ins)])


def shaped(*shape, dtype=F32):
    return jax.ShapeDtypeStruct(shape, dtype)


LISTED = pltpu.SMEM((LINES_HERE * SEGMENT + 1,), jnp.int32)


def per_device(vector, lengths, north_of, diagonal, lifting, inverse_rows):
    edge = shaped(MOVING, FACE, R, dtype=BF16)
    side = shaped(SEGMENT, FACE, R, dtype=BF16)
    blocks = shaped(LINES_HERE, SEGMENT, FACE, BLOCK, dtype=BF16)
    over_core, over_y, over_pair, over_next, steps, prefixes, last_two, whole, lower, inverse, vector, tile, alive = call(
        edges_kernel,
        (
            edge,
            edge,
            side,
            side,
            shaped(MOVING, SEGMENT, FACE, FACE),
            shaped(MOVING, SEGMENT - 1, FACE, FACE),
            shaped(MOVING, FACE, FACE),
            shaped(FACE, R),
            blocks,
            blocks,
            shaped(LINES_HERE, SEGMENT, BLOCK, R, dtype=BF16),
            shaped(16, HALF),
            shaped(LINES_HERE, SEGMENT, 8, HALF),
        ),
        (lengths, north_of, vector, lifting, inverse_rows),
        (
            pltpu.SMEM((LINES_HERE,), jnp.int32),
            pltpu.SMEM((1, LINES_HERE), jnp.int32),
            pltpu.SemaphoreType.DMA((2,)),
            pltpu.SemaphoreType.DMA((3, LINES_HERE)),
        ),
        in_hbm=(0, 1, 2, 3, 4),
    )
    walls, surfs = lax.axis_size(WALL), lax.axis_size(SURF)
    swap = [(0, 1), (1, 0)]
    over_core = lax.ppermute(over_core, "core", swap)
    rungs = [(i, i + 1) for i in range(1, walls - 1, 2)]
    over_y = lax.ppermute(over_y, WALL, rungs + [(b, a) for a, b in rungs])
    over_pair = lax.ppermute(over_pair, SURF, [(i, i ^ 1) for i in range(surfs)])
    nexts = [(i, (i + 1) % surfs) for i in range(1, surfs, 2)]
    over_next = lax.ppermute(over_next, SURF, nexts + [(b, a) for a, b in nexts])

    map_y = lax.ppermute(whole, "y", [(1, 0), (2, 3)])
    product, traces, squares = call(
        diagonal_kernel,
        (
            shaped(LINES_HERE, SEGMENT, BLOCK, R),
            shaped(LINES_HERE, SEGMENT, 6, FACE, R, dtype=BF16),
            shaped(8, R),
        ),
        (tile, vector, diagonal),
        (LISTED, pltpu.VMEM((2, BLOCK, HALF), F32)),
    )
    product, carries, outgoing = call(
        product_kernel,
        (
            shaped(LINES_HERE, SEGMENT, BLOCK, R),
            shaped(MOVING, SEGMENT - 1, FACE, R),
            shaped(MOVING + 2, FACE, R),
        ),
        (
            tile,
            traces,
            over_core,
            over_y,
            over_pair,
            over_next,
            lifting,
            inverse,
            steps,
            last_two,
            whole,
            map_y,
            product,
        ),
        (LISTED, pltpu.VMEM((LINES_HERE, SEGMENT, FACE, R), F32)),
    )
    ranks = lax.axis_size("y")

    def up_chips(value, far):
        return lax.ppermute(value, "y", [(i, i + far) for i in range(ranks - far)])

    beside = lax.ppermute(outgoing, "core", swap)
    near, far = call(chip_kernel, (shaped(MOVING, FACE, HALF), shaped(MOVING, FACE, HALF)), (outgoing, beside))
    one, two, three = up_chips(near, 1), up_chips(far, 2), up_chips(far, 3)
    arriving = call(arriving_kernel, shaped(MOVING, FACE, HALF), (one, two, three, outgoing, beside))
    arriving_beside = lax.ppermute(arriving, "core", swap)
    eliminated, tiles = call(
        eliminate_kernel,
        (shaped(LINES_HERE, SEGMENT, BLOCK, R), shaped(surfs, 8, HALF)),
        (tile, vector, squares, product, lower, prefixes, carries, arriving, arriving_beside, beside),
        (LISTED, pltpu.VMEM((LINES_HERE, SEGMENT, FACE, R), F32), pltpu.VMEM((2, 8, R), F32)),
        flops=10**9,
        moved=10**7,
    )
    tiles = lax.all_to_all(tiles, SURF, 0, 0, tiled=True)
    tiles = call(merge_kernel, shaped(walls, 8, HALF), (tiles,))
    tiles = lax.all_to_all(tiles, WALL, 0, 0, tiled=True)
    entries = LINES_HERE * SEGMENT * BLOCK * walls * surfs
    return call(
        functools.partial(finish_kernel, entries),
        (shaped(LINES_HERE, SEGMENT, BLOCK, R, dtype=BF16), shaped(2, R)),
        (alive, tiles, vector, eliminated),
        (pltpu.VMEM((LINES_HERE, SEGMENT, BLOCK, R), BF16), pltpu.SemaphoreType.DMA((LINES_HERE,))),
        out_specs=(pl.BlockSpec(memory_space=pl.ANY), in_vmem()),
    )


def solution(mesh):
    split = Mesh(mesh.devices.reshape(4, 2, 4, 8), ("y", "core", "x", "z"))
    placed = (
        P(SURF, WALL, None, None),
        P(SURF),
        P(SURF, None),
        P(SURF, WALL, None, None),
        P(SURF, WALL, None, None, None),
        P(SURF, WALL, None, None),
    )
    return jax.shard_map(
        per_device,
        mesh=split,
        in_specs=placed,
        out_specs=(P(SURF, WALL, None, None), P()),
        check_vma=False,
    )
```
